32 devices in a mesh: rc: 16 (over z, x, core), sys: 2 (over y).
Axes of the slice: x: 2, y: 2, z: 4, core: 2. Of those that a mesh axis runs over, the one named last changes fastest.
Arguments:
- density: bfloat16 [2, 64, 1600, 512], P(None, 'sys', 'rc'), may hold values from -6 to 6
- system_real: bfloat16 [64, 64], replicated, may hold values from -0.75 to 0.75
- system_imag: bfloat16 [64, 64], replicated, may hold values from -0.75 to 0.75
- left_ham: bfloat16 [40, 40], replicated, may hold values from -1 to 1
- left_coupling: bfloat16 [40, 40], replicated, may hold values from -1 to 1
- right_ham: bfloat16 [40, 40], replicated, may hold values from -1 to 1
- right_coupling: bfloat16 [40, 40], replicated, may hold values from -1 to 1
- left_strength: float32 [64], replicated, may hold values from -1.5 to 1.5
- right_strength: float32 [64], replicated, may hold values from -1.5 to 1.5
- left_damping: float32 [40], replicated, may hold values from 0.1 to 2
- right_damping: float32 [40], replicated, may hold values from 0.1 to 2
- energies: float32 [512], replicated, may hold values from -3 to 3
Outputs:
- derivative: bfloat16 [2, 64, 1600, 512], P(None, 'sys', 'rc')
The draws below stay inside these ranges and needn't reach their ends.
All inputs are finite; a program needn't handle non-finite values.
Results may differ from the reference program's by a relative error of at most 0.0047.
Values may be sent and summed in bfloat16 or wider, within the bound.
A program may use at most 192 MiB of HBM per device.

```python
import math
import jax
import jax.numpy as jnp
from jax import lax

S = 64
LEV = 40
PAIRS = 1600
COLS = 512


def shard_levels(key, extent, split, low, top_value):
    gain = 1.0
    for dim, parts in split:
        heights = jax.random.uniform(jax.random.fold_in(jax.random.fold_in(key, 6), dim), (parts,), jnp.float32, low / len(split), top_value / len(split))
        gain = gain * jnp.repeat(jnp.exp(heights), extent[dim] // parts).reshape((-1,) + (1,) * (len(extent) - 1 - dim))
    return gain


def normal_values(rng, extent, width, reach, shards=(), held_as=jnp.bfloat16):
    values = jax.random.normal(rng, extent, jnp.float32) * width
    if len(shards) > 0:
        values = shard_levels(rng, extent, shards, -0.22, 0.18) * values
    return jnp.clip(values, min=-reach, max=reach).astype(held_as)


def setup_inputs(seed: int = 0) -> dict:
    key_of = jax.random.split(jax.random.key(seed), 13)
    return {
        "density": normal_values(key_of[0], (2, S, PAIRS, COLS), 1.0, 6.0, ((1, 2), (2, 16))),
        "system_real": normal_values(key_of[1], (S, S), S ** -0.5, 0.75),
        "system_imag": normal_values(key_of[2], (S, S), S ** -0.5, 0.75),
        "left_ham": normal_values(key_of[3], (LEV, LEV), LEV ** -0.5, 1.0),
        "left_coupling": normal_values(key_of[4], (LEV, LEV), LEV ** -0.5, 1.0),
        "right_ham": normal_values(key_of[5], (LEV, LEV), LEV ** -0.5, 1.0),
        "right_coupling": normal_values(key_of[6], (LEV, LEV), LEV ** -0.5, 1.0),
        "left_strength": jnp.clip(jax.random.uniform(key_of[7], (S,), jnp.float32, -1.5, 1.5), -1.5, 1.5),
        "right_strength": jnp.clip(jax.random.uniform(key_of[8], (S,), jnp.float32, -1.5, 1.5), -1.5, 1.5),
        "left_damping": jnp.clip(jnp.exp(jax.random.uniform(key_of[9], (LEV,), jnp.float32, math.log(0.1), math.log(2.0))), 0.1, 2.0),
        "right_damping": jnp.clip(jnp.exp(jax.random.uniform(key_of[10], (LEV,), jnp.float32, math.log(0.1), math.log(2.0))), 0.1, 2.0),
        "energies": jnp.clip(jax.random.uniform(key_of[11], (COLS,), jnp.float32, -3.0, 3.0), -3.0, 3.0),
    }


def symmetric(matrix, factor):
    widened = matrix.astype(jnp.float32)
    return ((widened + factor * widened.T) * 0.5).astype(jnp.bfloat16)


def ladder_terms(block_rows, left_ops, right_ops, left_gain, right_gain):
    item_count, state_count, pair_count, column_count = block_rows.shape
    levels = left_ops.shape[1]
    widened = block_rows.reshape(item_count, state_count, levels, levels * column_count).astype(jnp.float32)
    left_all = jnp.einsum("xa,ksam->ksxm", left_ops.astype(jnp.float32), widened, precision=lax.Precision.HIGHEST)
    left_term = left_all[:, :, :levels] + left_gain[None, :, None, None] * left_all[:, :, levels:]
    deepened = block_rows.reshape(item_count, state_count, levels, levels, column_count).astype(jnp.float32)
    right_all = jnp.einsum("yb,ksabc->ksayc", right_ops.astype(jnp.float32), deepened, precision=lax.Precision.HIGHEST)
    right_term = right_all[:, :, :, :levels] + right_gain[None, :, None, None, None] * right_all[:, :, :, levels:]
    summed = left_term.reshape(item_count, state_count, pair_count, column_count) + right_term.reshape(item_count, state_count, pair_count, column_count)
    return summed.astype(jnp.bfloat16)


def reference(density, system_real, system_imag, left_ham, left_coupling, right_ham, right_coupling, left_strength, right_strength, left_damping, right_damping, energies):
    herm_real = symmetric(system_real, 1.0)
    herm_imag = symmetric(system_imag, -1.0)
    left_ops = jnp.concatenate([symmetric(left_ham, 1.0), symmetric(left_coupling, 1.0)], axis=0)
    right_ops = jnp.concatenate([symmetric(right_ham, 1.0), symmetric(right_coupling, 1.0)], axis=0)
    damping = (0.5 * (left_damping[:, None] + right_damping[None, :])).reshape(PAIRS)
    block_width = math.gcd(COLS, 128)
    block_count = COLS // block_width
    slabs = jnp.moveaxis(density.reshape(2, S, PAIRS, block_count, block_width), 3, 0)
    column_energy = energies.reshape(block_count, block_width)

    def one_block(inputs):
        block_rows, energy_row = inputs
        flattened = block_rows.reshape(2, S, PAIRS * block_width)
        real_part = jnp.dot(herm_real, flattened[0], preferred_element_type=jnp.float32) - jnp.dot(herm_imag, flattened[1], preferred_element_type=jnp.float32)
        imag_part = jnp.dot(herm_real, flattened[1], preferred_element_type=jnp.float32) + jnp.dot(herm_imag, flattened[0], preferred_element_type=jnp.float32)
        system_term = jnp.stack([real_part, imag_part]).astype(jnp.bfloat16).reshape(block_rows.shape).astype(jnp.float32)
        ladder = ladder_terms(block_rows, left_ops, right_ops, left_strength, right_strength).astype(jnp.float32)
        real_in = block_rows[0].astype(jnp.float32)
        imag_in = block_rows[1].astype(jnp.float32)
        energy_grid = energy_row[None, None, :]
        damp_grid = damping[None, :, None]
        new_real = ((system_term[1] + ladder[1]) - energy_grid * imag_in) - damp_grid * real_in
        new_imag = ((-system_term[0] - ladder[0]) + energy_grid * real_in) - damp_grid * imag_in
        return jnp.stack([new_real, new_imag]).astype(jnp.bfloat16)

    result = lax.map(one_block, (slabs, column_energy))
    return jnp.moveaxis(result, 0, 3).reshape(2, S, PAIRS, COLS)
```

```python
import functools
import math

import jax
import jax.numpy as jnp
from jax import lax
from jax.experimental import pallas as pl
from jax.experimental.pallas import tpu as pltpu
from jax.sharding import PartitionSpec as P

ROWS = 16
LANES = 128
STEP = 5


def symmetric(matrix, factor):
    widened = matrix.astype(jnp.float32)
    return ((widened + factor * widened.T) * 0.5).astype(jnp.bfloat16)


def ladder_local(regrouped, left_ops, right_ops, left_gain, right_gain, levels):
    item_count, group_count, all_pairs, column_count = regrouped.shape
    widened = regrouped.reshape(item_count, group_count, levels, levels * column_count)
    left_all = jnp.einsum("xa,ksam->ksxm", left_ops, widened, preferred_element_type=jnp.float32)
    left_term = left_all[:, :, :levels] + left_gain[None, :, None, None] * left_all[:, :, levels:]
    deepened = regrouped.reshape(item_count, group_count, levels, levels, column_count)
    right_all = jnp.einsum(
        "yb,ksabc->ksayc", right_ops, deepened, preferred_element_type=jnp.float32
    )
    right_term = (
        right_all[:, :, :, :levels]
        + right_gain[None, :, None, None, None] * right_all[:, :, :, levels:]
    )
    summed = left_term.reshape(
        item_count, group_count, all_pairs, column_count
    ) + right_term.reshape(item_count, group_count, all_pairs, column_count)
    return summed.astype(jnp.bfloat16)


def shards(
    density,
    system_real,
    system_imag,
    left_ham,
    left_coupling,
    right_ham,
    right_coupling,
    left_strength,
    right_strength,
    left_damping,
    right_damping,
    energies,
):
    herm_real = symmetric(system_real, 1.0)
    herm_imag = symmetric(system_imag, -1.0)
    levels = left_ham.shape[0]
    left_ops = jnp.concatenate([symmetric(left_ham, 1.0), symmetric(left_coupling, 1.0)], axis=0)
    right_ops = jnp.concatenate([symmetric(right_ham, 1.0), symmetric(right_coupling, 1.0)], axis=0)
    state_count = density.shape[1]
    pair_count = density.shape[2]
    column_total = density.shape[3]
    first_state = lax.axis_index("sys") * state_count
    left_gain = lax.dynamic_slice_in_dim(left_strength, first_state, state_count)
    right_gain = lax.dynamic_slice_in_dim(right_strength, first_state, state_count)
    regrouped = lax.all_to_all(density, "sys", split_axis=3, concat_axis=1, tiled=True)
    flattened = regrouped.reshape(2, regrouped.shape[1], -1)
    real_part = jnp.dot(herm_real, flattened[0], preferred_element_type=jnp.float32) - jnp.dot(
        herm_imag, flattened[1], preferred_element_type=jnp.float32
    )
    imag_part = jnp.dot(herm_real, flattened[1], preferred_element_type=jnp.float32) + jnp.dot(
        herm_imag, flattened[0], preferred_element_type=jnp.float32
    )
    product = jnp.stack([real_part, imag_part]).astype(jnp.bfloat16).reshape(regrouped.shape)
    system_rows = lax.all_to_all(product, "sys", split_axis=1, concat_axis=3, tiled=True)
    rc_count = lax.axis_size("rc")
    col_groups = rc_count // math.gcd(state_count, rc_count)
    per_device = state_count * col_groups // rc_count
    group_width = column_total // col_groups
    combined = jnp.moveaxis(
        density.reshape(2, state_count, pair_count, col_groups, group_width), 3, 2
    )
    combined = combined.reshape(2, state_count * col_groups, pair_count, group_width)
    combo_index = lax.axis_index("rc") * per_device + jnp.arange(per_device, dtype=jnp.int32)
    state_pick = (
        (combo_index // col_groups)[:, None] == jnp.arange(state_count, dtype=jnp.int32)[None, :]
    ).astype(jnp.float32)
    combo_left = jnp.sum(state_pick * left_gain[None, :], axis=1)
    combo_right = jnp.sum(state_pick * right_gain[None, :], axis=1)
    summed = ladder_local(
        lax.all_to_all(combined, "rc", split_axis=1, concat_axis=2, tiled=True),
        left_ops,
        right_ops,
        combo_left,
        combo_right,
        levels,
    )
    returned = lax.all_to_all(summed, "rc", split_axis=2, concat_axis=1, tiled=True)
    returned = returned.reshape(2, state_count, col_groups, pair_count, group_width)
    ladder_rows = jnp.moveaxis(returned, 2, 3).reshape(2, state_count, pair_count, column_total)
    pair_index = lax.axis_index("rc") * pair_count + jnp.arange(pair_count, dtype=jnp.int32)
    level_index = jnp.arange(levels, dtype=jnp.int32)
    left_pick = (pair_index[:, None] // levels == level_index[None, :]).astype(jnp.float32)
    right_pick = (pair_index[:, None] % levels == level_index[None, :]).astype(jnp.float32)
    damping = 0.5 * (
        jnp.sum(left_pick * left_damping[None, :], axis=1)
        + jnp.sum(right_pick * right_damping[None, :], axis=1)
    )
    system_term = system_rows.astype(jnp.float32)
    ladder = ladder_rows.astype(jnp.float32)
    real_in = density[0].astype(jnp.float32)
    imag_in = density[1].astype(jnp.float32)
    energy_grid = energies[None, None, :]
    damp_grid = damping[None, :, None]
    new_real = system_term[1] + ladder[1] - energy_grid * imag_in - damp_grid * real_in
    new_imag = -system_term[0] - ladder[0] + energy_grid * real_in - damp_grid * imag_in
    return jnp.stack([new_real, new_imag]).astype(jnp.bfloat16)


def one_hot(shape, hit):
    row = lax.broadcasted_iota(jnp.int32, shape, 0)
    col = lax.broadcasted_iota(jnp.int32, shape, 1)
    return jnp.where(hit(row, col), 1.0, 0.0).astype(jnp.bfloat16)


def product(left, right):
    return jnp.dot(left, right, preferred_element_type=jnp.float32)


def picked(left, right):
    return product(left, right).astype(jnp.bfloat16)


def symmetric_tile(matrix, factor):
    size = matrix.shape[0]
    eye = one_hot((size, size), lambda row, col: row == col)
    turned = lax.dot_general(
        matrix, eye, (((0,), (0,)), ((), ())), preferred_element_type=jnp.float32
    )
    return ((matrix.astype(jnp.float32) + factor * turned) * 0.5).astype(jnp.bfloat16)


def ladder_matrix(ham, coupling, strength, first_state):
    levels = ham.shape[0]
    size = levels * ROWS
    tall = one_hot((size, levels), lambda row, col: row // ROWS == col)
    wide = one_hot((levels, size), lambda row, col: row == col // ROWS)
    ham_all = product(picked(tall, symmetric_tile(ham, 1.0)), wide)
    coupling_all = product(picked(tall, symmetric_tile(coupling, 1.0)), wide)
    states = strength.shape[1]
    row = lax.broadcasted_iota(jnp.int32, (size, states), 0)
    col = lax.broadcasted_iota(jnp.int32, (size, states), 1)
    gain = jnp.sum(
        jnp.where(col == first_state + row % ROWS, strength, 0.0), axis=1, keepdims=True
    )
    row = lax.broadcasted_iota(jnp.int32, (size, size), 0)
    col = lax.broadcasted_iota(jnp.int32, (size, size), 1)
    mixed = ham_all + gain * coupling_all
    return jnp.where(row % ROWS == col % ROWS, mixed, 0.0).astype(jnp.bfloat16)


def system_matrix(system_real, system_imag, sys_index, local):
    states = system_real.shape[0]
    rows = one_hot((local, states), lambda row, col: col == row + local * sys_index)
    real = picked(rows, symmetric_tile(system_real, 1.0))
    imag = picked(rows, symmetric_tile(system_imag, -1.0))

    def place(part):
        def hit(row, col):
            block = col // local
            side = jnp.where(block < 2, sys_index, 1 - sys_index)
            return (block % 2 == part) & (row == col % local + local * side)

        return one_hot((states, 2 * states), hit)

    to_real, to_imag = place(0), place(1)
    upper = product(imag, to_real) + product(real, to_imag)
    lower = product(imag, to_imag) - product(real, to_real)
    return jnp.concatenate([upper, lower], axis=0).astype(jnp.bfloat16)


def section_kernel(
    count,
    dens,
    system_real,
    system_imag,
    left_ham,
    left_coupling,
    right_ham,
    right_coupling,
    left_strength,
    right_strength,
    left_damping,
    right_damping,
    energies,
    rest_out,
    left_out,
    mine,
    other,
    level,
    taken,
    given,
    rest,
    left_mat,
    right_mat,
    sys_mat,
    fwd_send,
    fwd_recv,
    ret_send,
    ret_recv,
    sys_send,
    sys_recv,
    level_sem,
    mine_sem,
    out_sem,
):
    me = lax.axis_index("rc")
    sys_index = lax.axis_index("sys")
    _, halves, half, local, columns = dens.shape
    levels = 2 * half
    row_blocks, lane_blocks = local // ROWS, columns // LANES
    chunks = half // STEP
    odd = lax.rem(me, 2)
    partner = me + 1 - 2 * odd
    shared = (halves - 1) * (1 - odd)

    def task(rank):
        part = rank // (row_blocks * lane_blocks)
        row = lax.rem(rank // lane_blocks, row_blocks) * ROWS
        lane = lax.rem(rank, lane_blocks) * LANES
        return part, pl.ds(pl.multiple_of(row, ROWS), ROWS), pl.ds(pl.multiple_of(lane, LANES), LANES)

    def peer(offset):
        return lax.rem(me + offset, count)

    def part_of(rank, chunk):
        part, row, lane = task(rank)
        return dens.at[part, :, pl.ds(chunk * STEP, STEP), row, lane]

    def forward(chunk, rank, owner):
        return pltpu.make_async_remote_copy(
            src_ref=part_of(rank, chunk),
            dst_ref=taken.at[chunk, pl.ds(owner * halves, halves)],
            send_sem=fwd_send.at[chunk, rank],
            recv_sem=fwd_recv.at[chunk, owner],
            device_id={"rc": rank},
            device_id_type=pl.DeviceIdType.MESH,
        )

    def forward_own(chunk):
        return pltpu.make_async_copy(
            part_of(me, chunk), taken.at[chunk, pl.ds(me * halves, halves)], fwd_recv.at[chunk, me]
        )

    def landing(rank, chunk):
        part, row, lane = task(rank)
        return left_out.at[1 - part, :, pl.ds(chunk * STEP, STEP), row, lane]

    def giveback(chunk, rank, worker):
        return pltpu.make_async_remote_copy(
            src_ref=given.at[chunk, pl.ds(rank * halves, halves)],
            dst_ref=landing(worker, chunk),
            send_sem=ret_send.at[chunk, rank],
            recv_sem=ret_recv.at[chunk, worker],
            device_id={"rc": rank},
            device_id_type=pl.DeviceIdType.MESH,
        )

    def giveback_own(chunk):
        return pltpu.make_async_copy(
            given.at[chunk, pl.ds(me * halves, halves)], landing(me, chunk), ret_recv.at[chunk, me]
        )

    def swap(index):
        return pltpu.make_async_remote_copy(
            src_ref=dens.at[:, index],
            dst_ref=other.at[:, index],
            send_sem=sys_send.at[index],
            recv_sem=sys_recv.at[index],
            device_id={"sys": 1 - sys_index},
            device_id_type=pl.DeviceIdType.MESH,
        )

    barrier = pltpu.get_barrier_semaphore()

    @pl.loop(1, count)
    def _(offset):
        pl.semaphore_signal(
            barrier, inc=1, device_id={"rc": peer(offset)}, device_id_type=pl.DeviceIdType.MESH
        )

    pl.semaphore_signal(
        barrier, inc=1, device_id={"sys": 1 - sys_index}, device_id_type=pl.DeviceIdType.MESH
    )
    pl.semaphore_wait(barrier, count)

    level_copy = pltpu.make_async_remote_copy(
        src_ref=dens.at[:, shared],
        dst_ref=level.at[:, odd],
        send_sem=level_sem.at[0],
        recv_sem=level_sem.at[1],
        device_id={"rc": partner},
        device_id_type=pl.DeviceIdType.MESH,
    )
    level_copy.start()
    level_own = pltpu.make_async_copy(dens.at[:, shared], level.at[:, odd], level_sem.at[2])
    level_own.start()
    mine_copy = pltpu.make_async_copy(dens, mine, mine_sem)
    mine_copy.start()

    @pl.loop(0, chunks)
    def _(chunk):
        forward_own(chunk).start()

        @pl.loop(1, count)
        def _(offset):
            forward(chunk, peer(offset), me).start()

    @pl.loop(0, halves)
    def _(index):
        swap(index).start()

    my_part = me // (row_blocks * lane_blocks)
    my_row = lax.rem(me // lane_blocks, row_blocks) * ROWS
    left_mat[...] = ladder_matrix(
        left_ham[...], left_coupling[...], left_strength[...], sys_index * local + my_row
    )
    for block in range(row_blocks):
        right_mat[block] = ladder_matrix(
            right_ham[...],
            right_coupling[...],
            right_strength[...],
            sys_index * local + block * ROWS,
        )
    sys_mat[...] = system_matrix(system_real[...], system_imag[...], sys_index, local)

    mine_copy.wait()
    level_own.wait()
    level_copy.wait()
    full_levels = halves // 2

    @pl.loop(0, 2)
    def _(part):
        sign = jnp.where(part == 1, 1.0, -1.0)
        for block in range(row_blocks):
            row = pl.ds(block * ROWS, ROWS)

            @pl.loop(0, full_levels)
            def _(number):
                first = odd + 2 * number
                held = mine[part, pl.ds(first, 2), :, row, :].reshape(levels * ROWS, columns)
                term = product(right_mat[block], held) * sign
                rest[1 - part, pl.ds(first, 2), :, row, :] = term.reshape(2, half, ROWS, columns)

            held = level[part, :, :, row, :].reshape(levels * ROWS, columns)
            rows = pl.ds(pl.multiple_of(odd * half * ROWS, half * ROWS), half * ROWS)
            term = product(right_mat[block, rows, :], held) * sign
            rest[1 - part, shared, :, row, :] = term.reshape(half, ROWS, columns)

    my_sign = jnp.where(my_part == 1, 1.0, -1.0)

    @pl.loop(0, chunks)
    def _(chunk):
        forward_own(chunk).wait()

        @pl.loop(1, count)
        def _(offset):
            forward(chunk, me, peer(offset)).wait_recv()

        for side in range(2):
            held = jnp.concatenate(
                [
                    jnp.concatenate(
                        [taken[chunk, 2 * number + side, at] for number in range(levels)], axis=0
                    )
                    for at in range(STEP)
                ],
                axis=1,
            )
            term = (product(left_mat[...], held) * my_sign).astype(jnp.bfloat16)
            for at in range(STEP):
                for number in range(levels):
                    given[chunk, 2 * number + side, at] = term[
                        number * ROWS : (number + 1) * ROWS, at * LANES : (at + 1) * LANES
                    ]
        giveback_own(chunk).start()

        @pl.loop(1, count)
        def _(offset):
            giveback(chunk, peer(offset), me).start()

    @pl.loop(0, halves)
    def _(index):
        swap(index).wait_recv()

        @pl.loop(0, half)
        def _(at):
            pair = (me * halves + index) * half + at
            damping = 0.5 * (left_damping[pair // levels] + right_damping[lax.rem(pair, levels)])
            real, imag = mine[0, index, at], mine[1, index, at]
            held = jnp.concatenate([real, imag, other[0, index, at], other[1, index, at]], axis=0)
            term = product(sys_mat[...], held)
            real, imag = real.astype(jnp.float32), imag.astype(jnp.float32)
            energy = energies[...]
            new_real = term[:local] + rest[0, index, at] - energy * imag - damping * real
            new_imag = term[local:] + rest[1, index, at] + energy * real - damping * imag
            other[0, index, at] = new_real.astype(jnp.bfloat16)
            other[1, index, at] = new_imag.astype(jnp.bfloat16)

        pltpu.make_async_copy(other.at[:, index], rest_out.at[:, index], out_sem.at[index]).start()

    @pl.loop(0, halves)
    def _(index):
        swap(index).wait_send()
        pltpu.make_async_copy(other.at[:, index], rest_out.at[:, index], out_sem.at[index]).wait()

    @pl.loop(0, chunks)
    def _(chunk):
        giveback_own(chunk).wait()

        @pl.loop(1, count)
        def _(offset):
            rank = peer(offset)
            forward(chunk, rank, me).wait_send()
            giveback(chunk, rank, me).wait_send()
            giveback(chunk, me, rank).wait_recv()


def exchanged(
    density,
    system_real,
    system_imag,
    left_ham,
    left_coupling,
    right_ham,
    right_coupling,
    left_strength,
    right_strength,
    left_damping,
    right_damping,
    energies,
):
    count = lax.axis_size("rc")
    levels = left_ham.shape[0]
    half = levels // 2
    _, local, pairs, columns = density.shape
    halves = pairs // half
    chunks = half // STEP
    size = levels * ROWS
    row_blocks = local // ROWS
    dens = jnp.transpose(density, (0, 2, 1, 3)).reshape(2, halves, half, local, columns)
    whole = pl.BlockSpec(memory_space=pltpu.VMEM)
    scalars = pl.BlockSpec(memory_space=pltpu.SMEM)
    anywhere = pl.BlockSpec(memory_space=pl.ANY)
    slab = jax.ShapeDtypeStruct(dens.shape, jnp.bfloat16)
    rest, left = pl.pallas_call(
        functools.partial(section_kernel, count),
        out_shape=[slab, slab],
        in_specs=[anywhere] + [whole] * 8 + [scalars] * 2 + [whole],
        out_specs=[anywhere, anywhere],
        scratch_shapes=[
            pltpu.VMEM(dens.shape, jnp.bfloat16),
            pltpu.VMEM(dens.shape, jnp.bfloat16),
            pltpu.VMEM((2, 2, half, local, columns), jnp.bfloat16),
            pltpu.VMEM((chunks, count * halves, STEP, ROWS, LANES), jnp.bfloat16),
            pltpu.VMEM((chunks, count * halves, STEP, ROWS, LANES), jnp.bfloat16),
            pltpu.VMEM(dens.shape, jnp.float32),
            pltpu.VMEM((size, size), jnp.bfloat16),
            pltpu.VMEM((row_blocks, size, size), jnp.bfloat16),
            pltpu.VMEM((2 * local, 4 * local), jnp.bfloat16),
            pltpu.SemaphoreType.DMA((chunks, count)),
            pltpu.SemaphoreType.DMA((chunks, count)),
            pltpu.SemaphoreType.DMA((chunks, count)),
            pltpu.SemaphoreType.DMA((chunks, count)),
            pltpu.SemaphoreType.DMA((halves,)),
            pltpu.SemaphoreType.DMA((halves,)),
            pltpu.SemaphoreType.DMA((3,)),
            pltpu.SemaphoreType.DMA,
            pltpu.SemaphoreType.DMA((halves,)),
        ],
        compiler_params=pltpu.CompilerParams(
            collective_id=0, has_side_effects=True, vmem_limit_bytes=60 * 2**20
        ),
        cost_estimate=pl.CostEstimate(
            flops=10 * 10**9, bytes_accessed=5 * dens.size * 2, transcendentals=0
        ),
    )(
        dens,
        system_real,
        system_imag,
        left_ham,
        left_coupling,
        right_ham,
        right_coupling,
        left_strength[None, :],
        right_strength[None, :],
        left_damping,
        right_damping,
        energies[None, :],
    )
    total = (rest.astype(jnp.float32) + left.astype(jnp.float32)).astype(jnp.bfloat16)
    return jnp.transpose(total.reshape(2, pairs, local, columns), (0, 2, 1, 3))


def fits(mesh, shapes):
    count, sides = mesh.shape["rc"], mesh.shape["sys"]
    _, states, pairs, columns = shapes[0]
    levels = shapes[3][0]
    if sides != 2 or levels % 2 or pairs % count or states % (2 * ROWS) or columns % LANES:
        return False
    half, local_pairs = levels // 2, pairs // count
    tasks = 2 * (states // (2 * ROWS)) * (columns // LANES)
    return (
        tasks == count
        and half % STEP == 0
        and local_pairs % half == 0
        and local_pairs // half % 2 == 1
    )


def solution(mesh):
    placed = (P(None, "sys", "rc", None), P(), P(), P(), P(), P(), P(), P(), P(), P(), P(), P())

    def run(*arrays):
        body = exchanged if fits(mesh, [array.shape for array in arrays]) else shards
        return jax.shard_map(
            body, mesh=mesh, in_specs=placed, out_specs=P(None, "sys", "rc", None), check_vma=False
        )(*arrays)

    return run
```

```python
import functools
import math

import jax
import jax.numpy as jnp
from jax import lax
from jax.experimental import pallas as pl
from jax.experimental.pallas import tpu as pltpu
from jax.sharding import PartitionSpec as P

ROWS = 16
LANES = 128
STEP = 5


def symmetric(matrix, factor):
    widened = matrix.astype(jnp.float32)
    return ((widened + factor * widened.T) * 0.5).astype(jnp.bfloat16)


def ladder_local(regrouped, left_ops, right_ops, left_gain, right_gain, levels):
    item_count, group_count, all_pairs, column_count = regrouped.shape
    widened = regrouped.reshape(item_count, group_count, levels, levels * column_count)
    left_all = jnp.einsum("xa,ksam->ksxm", left_ops, widened, preferred_element_type=jnp.float32)
    left_term = left_all[:, :, :levels] + left_gain[None, :, None, None] * left_all[:, :, levels:]
    deepened = regrouped.reshape(item_count, group_count, levels, levels, column_count)
    right_all = jnp.einsum(
        "yb,ksabc->ksayc", right_ops, deepened, preferred_element_type=jnp.float32
    )
    right_term = (
        right_all[:, :, :, :levels]
        + right_gain[None, :, None, None, None] * right_all[:, :, :, levels:]
    )
    summed = left_term.reshape(
        item_count, group_count, all_pairs, column_count
    ) + right_term.reshape(item_count, group_count, all_pairs, column_count)
    return summed.astype(jnp.bfloat16)


def shards(
    density,
    system_real,
    system_imag,
    left_ham,
    left_coupling,
    right_ham,
    right_coupling,
    left_strength,
    right_strength,
    left_damping,
    right_damping,
    energies,
):
    herm_real = symmetric(system_real, 1.0)
    herm_imag = symmetric(system_imag, -1.0)
    levels = left_ham.shape[0]
    left_ops = jnp.concatenate([symmetric(left_ham, 1.0), symmetric(left_coupling, 1.0)], axis=0)
    right_ops = jnp.concatenate([symmetric(right_ham, 1.0), symmetric(right_coupling, 1.0)], axis=0)
    state_count = density.shape[1]
    pair_count = density.shape[2]
    column_total = density.shape[3]
    first_state = lax.axis_index("sys") * state_count
    left_gain = lax.dynamic_slice_in_dim(left_strength, first_state, state_count)
    right_gain = lax.dynamic_slice_in_dim(right_strength, first_state, state_count)
    regrouped = lax.all_to_all(density, "sys", split_axis=3, concat_axis=1, tiled=True)
    flattened = regrouped.reshape(2, regrouped.shape[1], -1)
    real_part = jnp.dot(herm_real, flattened[0], preferred_element_type=jnp.float32) - jnp.dot(
        herm_imag, flattened[1], preferred_element_type=jnp.float32
    )
    imag_part = jnp.dot(herm_real, flattened[1], preferred_element_type=jnp.float32) + jnp.dot(
        herm_imag, flattened[0], preferred_element_type=jnp.float32
    )
    product = jnp.stack([real_part, imag_part]).astype(jnp.bfloat16).reshape(regrouped.shape)
    system_rows = lax.all_to_all(product, "sys", split_axis=1, concat_axis=3, tiled=True)
    rc_count = lax.axis_size("rc")
    col_groups = rc_count // math.gcd(state_count, rc_count)
    per_device = state_count * col_groups // rc_count
    group_width = column_total // col_groups
    combined = jnp.moveaxis(
        density.reshape(2, state_count, pair_count, col_groups, group_width), 3, 2
    )
    combined = combined.reshape(2, state_count * col_groups, pair_count, group_width)
    combo_index = lax.axis_index("rc") * per_device + jnp.arange(per_device, dtype=jnp.int32)
    state_pick = (
        (combo_index // col_groups)[:, None] == jnp.arange(state_count, dtype=jnp.int32)[None, :]
    ).astype(jnp.float32)
    combo_left = jnp.sum(state_pick * left_gain[None, :], axis=1)
    combo_right = jnp.sum(state_pick * right_gain[None, :], axis=1)
    summed = ladder_local(
        lax.all_to_all(combined, "rc", split_axis=1, concat_axis=2, tiled=True),
        left_ops,
        right_ops,
        combo_left,
        combo_right,
        levels,
    )
    returned = lax.all_to_all(summed, "rc", split_axis=2, concat_axis=1, tiled=True)
    returned = returned.reshape(2, state_count, col_groups, pair_count, group_width)
    ladder_rows = jnp.moveaxis(returned, 2, 3).reshape(2, state_count, pair_count, column_total)
    pair_index = lax.axis_index("rc") * pair_count + jnp.arange(pair_count, dtype=jnp.int32)
    level_index = jnp.arange(levels, dtype=jnp.int32)
    left_pick = (pair_index[:, None] // levels == level_index[None, :]).astype(jnp.float32)
    right_pick = (pair_index[:, None] % levels == level_index[None, :]).astype(jnp.float32)
    damping = 0.5 * (
        jnp.sum(left_pick * left_damping[None, :], axis=1)
        + jnp.sum(right_pick * right_damping[None, :], axis=1)
    )
    system_term = system_rows.astype(jnp.float32)
    ladder = ladder_rows.astype(jnp.float32)
    real_in = density[0].astype(jnp.float32)
    imag_in = density[1].astype(jnp.float32)
    energy_grid = energies[None, None, :]
    damp_grid = damping[None, :, None]
    new_real = system_term[1] + ladder[1] - energy_grid * imag_in - damp_grid * real_in
    new_imag = -system_term[0] - ladder[0] + energy_grid * real_in - damp_grid * imag_in
    return jnp.stack([new_real, new_imag]).astype(jnp.bfloat16)


def one_hot(shape, hit):
    row = lax.broadcasted_iota(jnp.int32, shape, 0)
    col = lax.broadcasted_iota(jnp.int32, shape, 1)
    return jnp.where(hit(row, col), 1.0, 0.0).astype(jnp.bfloat16)


def product(left, right):
    return jnp.dot(left, right, preferred_element_type=jnp.float32)


def picked(left, right):
    return product(left, right).astype(jnp.bfloat16)


def symmetric_tile(matrix, factor):
    size = matrix.shape[0]
    eye = one_hot((size, size), lambda row, col: row == col)
    turned = lax.dot_general(
        matrix, eye, (((0,), (0,)), ((), ())), preferred_element_type=jnp.float32
    )
    return ((matrix.astype(jnp.float32) + factor * turned) * 0.5).astype(jnp.bfloat16)


def ladder_matrix(ham, coupling, strength, first_state):
    levels = ham.shape[0]
    size = levels * ROWS
    tall = one_hot((size, levels), lambda row, col: row // ROWS == col)
    wide = one_hot((levels, size), lambda row, col: row == col // ROWS)
    ham_all = product(picked(tall, symmetric_tile(ham, 1.0)), wide)
    coupling_all = product(picked(tall, symmetric_tile(coupling, 1.0)), wide)
    states = strength.shape[1]
    row = lax.broadcasted_iota(jnp.int32, (size, states), 0)
    col = lax.broadcasted_iota(jnp.int32, (size, states), 1)
    gain = jnp.sum(
        jnp.where(col == first_state + row % ROWS, strength, 0.0), axis=1, keepdims=True
    )
    row = lax.broadcasted_iota(jnp.int32, (size, size), 0)
    col = lax.broadcasted_iota(jnp.int32, (size, size), 1)
    mixed = ham_all + gain * coupling_all
    return jnp.where(row % ROWS == col % ROWS, mixed, 0.0).astype(jnp.bfloat16)


def system_matrix(system_real, system_imag, sys_index, local):
    states = system_real.shape[0]
    rows = one_hot((local, states), lambda row, col: col == row + local * sys_index)
    real = picked(rows, symmetric_tile(system_real, 1.0))
    imag = picked(rows, symmetric_tile(system_imag, -1.0))

    def place(part):
        def hit(row, col):
            block = col // local
            side = jnp.where(block < 2, sys_index, 1 - sys_index)
            return (block % 2 == part) & (row == col % local + local * side)

        return one_hot((states, 2 * states), hit)

    to_real, to_imag = place(0), place(1)
    upper = product(imag, to_real) + product(real, to_imag)
    lower = product(imag, to_imag) - product(real, to_real)
    return jnp.concatenate([upper, lower], axis=0).astype(jnp.bfloat16)


def section_kernel(
    count,
    dens,
    system_real,
    system_imag,
    left_ham,
    left_coupling,
    right_ham,
    right_coupling,
    left_strength,
    right_strength,
    left_damping,
    right_damping,
    energies,
    rest_out,
    left_out,
    mine,
    other,
    level,
    taken,
    given,
    rest,
    left_mat,
    right_mat,
    sys_mat,
    fwd_send,
    fwd_recv,
    ret_send,
    ret_recv,
    sys_send,
    sys_recv,
    level_sem,
    mine_sem,
    out_sem,
):
    me = lax.axis_index("rc")
    sys_index = lax.axis_index("sys")
    _, halves, half, local, columns = dens.shape
    levels = 2 * half
    row_blocks, lane_blocks = local // ROWS, columns // LANES
    chunks = half // STEP
    odd = lax.rem(me, 2)
    partner = me + 1 - 2 * odd
    shared = (halves - 1) * (1 - odd)

    def task(rank):
        part = rank // (row_blocks * lane_blocks)
        row = lax.rem(rank // lane_blocks, row_blocks) * ROWS
        lane = lax.rem(rank, lane_blocks) * LANES
        return part, pl.ds(pl.multiple_of(row, ROWS), ROWS), pl.ds(pl.multiple_of(lane, LANES), LANES)

    def peer(turn):
        side = count // 2
        other_side = lax.rem(turn, 2)
        return lax.rem(me // side + other_side, 2) * side + lax.rem(me + turn // 2, side)

    def part_of(rank, chunk):
        part, row, lane = task(rank)
        return dens.at[part, :, pl.ds(chunk * STEP, STEP), row, lane]

    def forward(chunk, rank, owner):
        return pltpu.make_async_remote_copy(
            src_ref=part_of(rank, chunk),
            dst_ref=taken.at[chunk, pl.ds(owner * halves, halves)],
            send_sem=fwd_send.at[chunk, rank],
            recv_sem=fwd_recv.at[chunk, owner],
            device_id={"rc": rank},
            device_id_type=pl.DeviceIdType.MESH,
        )

    def forward_own(chunk):
        return pltpu.make_async_copy(
            part_of(me, chunk), taken.at[chunk, pl.ds(me * halves, halves)], fwd_recv.at[chunk, me]
        )

    def landing(rank, chunk):
        part, row, lane = task(rank)
        return left_out.at[1 - part, :, pl.ds(chunk * STEP, STEP), row, lane]

    def giveback(chunk, rank, worker):
        return pltpu.make_async_remote_copy(
            src_ref=given.at[chunk, pl.ds(rank * halves, halves)],
            dst_ref=landing(worker, chunk),
            send_sem=ret_send.at[chunk, rank],
            recv_sem=ret_recv.at[chunk, worker],
            device_id={"rc": rank},
            device_id_type=pl.DeviceIdType.MESH,
        )

    def giveback_own(chunk):
        return pltpu.make_async_copy(
            given.at[chunk, pl.ds(me * halves, halves)], landing(me, chunk), ret_recv.at[chunk, me]
        )

    def swap(index):
        return pltpu.make_async_remote_copy(
            src_ref=dens.at[:, index],
            dst_ref=other.at[:, index],
            send_sem=sys_send.at[index],
            recv_sem=sys_recv.at[index],
            device_id={"sys": 1 - sys_index},
            device_id_type=pl.DeviceIdType.MESH,
        )

    barrier = pltpu.get_barrier_semaphore()

    @pl.loop(1, count)
    def _(offset):
        pl.semaphore_signal(
            barrier, inc=1, device_id={"rc": peer(offset)}, device_id_type=pl.DeviceIdType.MESH
        )

    pl.semaphore_signal(
        barrier, inc=1, device_id={"sys": 1 - sys_index}, device_id_type=pl.DeviceIdType.MESH
    )
    pl.semaphore_wait(barrier, count)

    level_copy = pltpu.make_async_remote_copy(
        src_ref=dens.at[:, shared],
        dst_ref=level.at[:, odd],
        send_sem=level_sem.at[0],
        recv_sem=level_sem.at[1],
        device_id={"rc": partner},
        device_id_type=pl.DeviceIdType.MESH,
    )
    level_copy.start()
    level_own = pltpu.make_async_copy(dens.at[:, shared], level.at[:, odd], level_sem.at[2])
    level_own.start()
    mine_copy = pltpu.make_async_copy(dens, mine, mine_sem)
    mine_copy.start()

    @pl.loop(0, chunks)
    def _(chunk):
        forward_own(chunk).start()

        @pl.loop(1, count)
        def _(offset):
            forward(chunk, peer(offset), me).start()

        swap(chunk).start()

    @pl.loop(chunks, halves)
    def _(index):
        swap(index).start()

    my_part = me // (row_blocks * lane_blocks)
    my_row = lax.rem(me // lane_blocks, row_blocks) * ROWS
    left_mat[...] = ladder_matrix(
        left_ham[...], left_coupling[...], left_strength[...], sys_index * local + my_row
    )
    for block in range(row_blocks):
        right_mat[block] = ladder_matrix(
            right_ham[...],
            right_coupling[...],
            right_strength[...],
            sys_index * local + block * ROWS,
        )
    sys_mat[...] = system_matrix(system_real[...], system_imag[...], sys_index, local)

    mine_copy.wait()
    level_own.wait()
    level_copy.wait()
    full_levels = halves // 2

    @pl.loop(0, 2)
    def _(part):
        sign = jnp.where(part == 1, 1.0, -1.0)
        for block in range(row_blocks):
            row = pl.ds(block * ROWS, ROWS)

            @pl.loop(0, full_levels)
            def _(number):
                first = odd + 2 * number
                held = mine[part, pl.ds(first, 2), :, row, :].reshape(levels * ROWS, columns)
                term = product(right_mat[block], held) * sign
                rest[1 - part, pl.ds(first, 2), :, row, :] = term.reshape(2, half, ROWS, columns)

            held = level[part, :, :, row, :].reshape(levels * ROWS, columns)
            rows = pl.ds(pl.multiple_of(odd * half * ROWS, half * ROWS), half * ROWS)
            term = product(right_mat[block, rows, :], held) * sign
            rest[1 - part, shared, :, row, :] = term.reshape(half, ROWS, columns)

    my_sign = jnp.where(my_part == 1, 1.0, -1.0)

    @pl.loop(0, chunks)
    def _(chunk):
        forward_own(chunk).wait()

        @pl.loop(1, count)
        def _(offset):
            forward(chunk, me, peer(offset)).wait_recv()

        for side in range(2):
            held = jnp.concatenate(
                [
                    jnp.concatenate(
                        [taken[chunk, 2 * number + side, at] for number in range(levels)], axis=0
                    )
                    for at in range(STEP)
                ],
                axis=1,
            )
            term = (product(left_mat[...], held) * my_sign).astype(jnp.bfloat16)
            for at in range(STEP):
                for number in range(levels):
                    given[chunk, 2 * number + side, at] = term[
                        number * ROWS : (number + 1) * ROWS, at * LANES : (at + 1) * LANES
                    ]
        giveback_own(chunk).start()

        @pl.loop(1, count)
        def _(offset):
            giveback(chunk, peer(offset), me).start()

    @pl.loop(0, halves)
    def _(index):
        swap(index).wait_recv()

        @pl.loop(0, half)
        def _(at):
            pair = (me * halves + index) * half + at
            damping = 0.5 * (left_damping[pair // levels] + right_damping[lax.rem(pair, levels)])
            real, imag = mine[0, index, at], mine[1, index, at]
            held = jnp.concatenate([real, imag, other[0, index, at], other[1, index, at]], axis=0)
            term = product(sys_mat[...], held)
            real, imag = real.astype(jnp.float32), imag.astype(jnp.float32)
            energy = energies[...]
            new_real = term[:local] + rest[0, index, at] - energy * imag - damping * real
            new_imag = term[local:] + rest[1, index, at] + energy * real - damping * imag
            other[0, index, at] = new_real.astype(jnp.bfloat16)
            other[1, index, at] = new_imag.astype(jnp.bfloat16)

        pltpu.make_async_copy(other.at[:, index], rest_out.at[:, index], out_sem.at[index]).start()

    @pl.loop(0, halves)
    def _(index):
        swap(index).wait_send()
        pltpu.make_async_copy(other.at[:, index], rest_out.at[:, index], out_sem.at[index]).wait()

    @pl.loop(0, chunks)
    def _(chunk):
        giveback_own(chunk).wait()

        @pl.loop(1, count)
        def _(offset):
            rank = peer(offset)
            forward(chunk, rank, me).wait_send()
            giveback(chunk, rank, me).wait_send()
            giveback(chunk, me, rank).wait_recv()


def add_kernel(rest, left, total):
    total[...] = (rest[...].astype(jnp.float32) + left[...].astype(jnp.float32)).astype(jnp.bfloat16)


def exchanged(
    density,
    system_real,
    system_imag,
    left_ham,
    left_coupling,
    right_ham,
    right_coupling,
    left_strength,
    right_strength,
    left_damping,
    right_damping,
    energies,
):
    count = lax.axis_size("rc")
    levels = left_ham.shape[0]
    half = levels // 2
    _, local, pairs, columns = density.shape
    halves = pairs // half
    chunks = half // STEP
    size = levels * ROWS
    row_blocks = local // ROWS
    dens = jnp.transpose(density, (0, 2, 1, 3)).reshape(2, halves, half, local, columns)
    whole = pl.BlockSpec(memory_space=pltpu.VMEM)
    scalars = pl.BlockSpec(memory_space=pltpu.SMEM)
    anywhere = pl.BlockSpec(memory_space=pl.ANY)
    slab = jax.ShapeDtypeStruct(dens.shape, jnp.bfloat16)
    rest, left = pl.pallas_call(
        functools.partial(section_kernel, count),
        out_shape=[slab, slab],
        in_specs=[anywhere] + [whole] * 8 + [scalars] * 2 + [whole],
        out_specs=[anywhere, anywhere],
        scratch_shapes=[
            pltpu.VMEM(dens.shape, jnp.bfloat16),
            pltpu.VMEM(dens.shape, jnp.bfloat16),
            pltpu.VMEM((2, 2, half, local, columns), jnp.bfloat16),
            pltpu.VMEM((chunks, count * halves, STEP, ROWS, LANES), jnp.bfloat16),
            pltpu.VMEM((chunks, count * halves, STEP, ROWS, LANES), jnp.bfloat16),
            pltpu.VMEM(dens.shape, jnp.float32),
            pltpu.VMEM((size, size), jnp.bfloat16),
            pltpu.VMEM((row_blocks, size, size), jnp.bfloat16),
            pltpu.VMEM((2 * local, 4 * local), jnp.bfloat16),
            pltpu.SemaphoreType.DMA((chunks, count)),
            pltpu.SemaphoreType.DMA((chunks, count)),
            pltpu.SemaphoreType.DMA((chunks, count)),
            pltpu.SemaphoreType.DMA((chunks, count)),
            pltpu.SemaphoreType.DMA((halves,)),
            pltpu.SemaphoreType.DMA((halves,)),
            pltpu.SemaphoreType.DMA((3,)),
            pltpu.SemaphoreType.DMA,
            pltpu.SemaphoreType.DMA((halves,)),
        ],
        compiler_params=pltpu.CompilerParams(
            collective_id=0, has_side_effects=True, vmem_limit_bytes=60 * 2**20
        ),
        cost_estimate=pl.CostEstimate(
            flops=10 * 10**9, bytes_accessed=5 * dens.size * 2, transcendentals=0
        ),
    )(
        dens,
        system_real,
        system_imag,
        left_ham,
        left_coupling,
        right_ham,
        right_coupling,
        left_strength[None, :],
        right_strength[None, :],
        left_damping,
        right_damping,
        energies[None, :],
    )
    block = pl.BlockSpec((1, 1, half, local, columns), lambda part, index: (part, index, 0, 0, 0))
    total = pl.pallas_call(
        add_kernel,
        out_shape=slab,
        grid=(2, halves),
        in_specs=[block, block],
        out_specs=block,
        cost_estimate=pl.CostEstimate(
            flops=dens.size, bytes_accessed=3 * dens.size * 2, transcendentals=0
        ),
    )(rest, left)
    return jnp.transpose(total.reshape(2, pairs, local, columns), (0, 2, 1, 3))


def fits(mesh, shapes):
    count, sides = mesh.shape["rc"], mesh.shape["sys"]
    _, states, pairs, columns = shapes[0]
    levels = shapes[3][0]
    if sides != 2 or levels % 2 or pairs % count or states % (2 * ROWS) or columns % LANES:
        return False
    half, local_pairs = levels // 2, pairs // count
    tasks = 2 * (states // (2 * ROWS)) * (columns // LANES)
    return (
        tasks == count
        and half % STEP == 0
        and local_pairs % half == 0
        and local_pairs // half % 2 == 1
        and local_pairs // half >= half // STEP
    )


def solution(mesh):
    placed = (P(None, "sys", "rc", None), P(), P(), P(), P(), P(), P(), P(), P(), P(), P(), P())

    def run(*arrays):
        body = exchanged if fits(mesh, [array.shape for array in arrays]) else shards
        return jax.shard_map(
            body, mesh=mesh, in_specs=placed, out_specs=P(None, "sys", "rc", None), check_vma=False
        )(*arrays)

    return run
```

```python
import functools
import math

import jax
import jax.numpy as jnp
from jax import lax
from jax.experimental import pallas as pl
from jax.experimental.pallas import tpu as pltpu
from jax.sharding import PartitionSpec as P

ROWS = 16
LANES = 128
STEP = 5


def symmetric(matrix, factor):
    widened = matrix.astype(jnp.float32)
    return ((widened + factor * widened.T) * 0.5).astype(jnp.bfloat16)


def ladder_local(regrouped, left_ops, right_ops, left_gain, right_gain, levels):
    item_count, group_count, all_pairs, column_count = regrouped.shape
    widened = regrouped.reshape(item_count, group_count, levels, levels * column_count)
    left_all = jnp.einsum("xa,ksam->ksxm", left_ops, widened, preferred_element_type=jnp.float32)
    left_term = left_all[:, :, :levels] + left_gain[None, :, None, None] * left_all[:, :, levels:]
    deepened = regrouped.reshape(item_count, group_count, levels, levels, column_count)
    right_all = jnp.einsum(
        "yb,ksabc->ksayc", right_ops, deepened, preferred_element_type=jnp.float32
    )
    right_term = (
        right_all[:, :, :, :levels]
        + right_gain[None, :, None, None, None] * right_all[:, :, :, levels:]
    )
    summed = left_term.reshape(
        item_count, group_count, all_pairs, column_count
    ) + right_term.reshape(item_count, group_count, all_pairs, column_count)
    return summed.astype(jnp.bfloat16)


def shards(
    density,
    system_real,
    system_imag,
    left_ham,
    left_coupling,
    right_ham,
    right_coupling,
    left_strength,
    right_strength,
    left_damping,
    right_damping,
    energies,
):
    herm_real = symmetric(system_real, 1.0)
    herm_imag = symmetric(system_imag, -1.0)
    levels = left_ham.shape[0]
    left_ops = jnp.concatenate([symmetric(left_ham, 1.0), symmetric(left_coupling, 1.0)], axis=0)
    right_ops = jnp.concatenate([symmetric(right_ham, 1.0), symmetric(right_coupling, 1.0)], axis=0)
    state_count = density.shape[1]
    pair_count = density.shape[2]
    column_total = density.shape[3]
    first_state = lax.axis_index("sys") * state_count
    left_gain = lax.dynamic_slice_in_dim(left_strength, first_state, state_count)
    right_gain = lax.dynamic_slice_in_dim(right_strength, first_state, state_count)
    regrouped = lax.all_to_all(density, "sys", split_axis=3, concat_axis=1, tiled=True)
    flattened = regrouped.reshape(2, regrouped.shape[1], -1)
    real_part = jnp.dot(herm_real, flattened[0], preferred_element_type=jnp.float32) - jnp.dot(
        herm_imag, flattened[1], preferred_element_type=jnp.float32
    )
    imag_part = jnp.dot(herm_real, flattened[1], preferred_element_type=jnp.float32) + jnp.dot(
        herm_imag, flattened[0], preferred_element_type=jnp.float32
    )
    product = jnp.stack([real_part, imag_part]).astype(jnp.bfloat16).reshape(regrouped.shape)
    system_rows = lax.all_to_all(product, "sys", split_axis=1, concat_axis=3, tiled=True)
    rc_count = lax.axis_size("rc")
    col_groups = rc_count // math.gcd(state_count, rc_count)
    per_device = state_count * col_groups // rc_count
    group_width = column_total // col_groups
    combined = jnp.moveaxis(
        density.reshape(2, state_count, pair_count, col_groups, group_width), 3, 2
    )
    combined = combined.reshape(2, state_count * col_groups, pair_count, group_width)
    combo_index = lax.axis_index("rc") * per_device + jnp.arange(per_device, dtype=jnp.int32)
    state_pick = (
        (combo_index // col_groups)[:, None] == jnp.arange(state_count, dtype=jnp.int32)[None, :]
    ).astype(jnp.float32)
    combo_left = jnp.sum(state_pick * left_gain[None, :], axis=1)
    combo_right = jnp.sum(state_pick * right_gain[None, :], axis=1)
    summed = ladder_local(
        lax.all_to_all(combined, "rc", split_axis=1, concat_axis=2, tiled=True),
        left_ops,
        right_ops,
        combo_left,
        combo_right,
        levels,
    )
    returned = lax.all_to_all(summed, "rc", split_axis=2, concat_axis=1, tiled=True)
    returned = returned.reshape(2, state_count, col_groups, pair_count, group_width)
    ladder_rows = jnp.moveaxis(returned, 2, 3).reshape(2, state_count, pair_count, column_total)
    pair_index = lax.axis_index("rc") * pair_count + jnp.arange(pair_count, dtype=jnp.int32)
    level_index = jnp.arange(levels, dtype=jnp.int32)
    left_pick = (pair_index[:, None] // levels == level_index[None, :]).astype(jnp.float32)
    right_pick = (pair_index[:, None] % levels == level_index[None, :]).astype(jnp.float32)
    damping = 0.5 * (
        jnp.sum(left_pick * left_damping[None, :], axis=1)
        + jnp.sum(right_pick * right_damping[None, :], axis=1)
    )
    system_term = system_rows.astype(jnp.float32)
    ladder = ladder_rows.astype(jnp.float32)
    real_in = density[0].astype(jnp.float32)
    imag_in = density[1].astype(jnp.float32)
    energy_grid = energies[None, None, :]
    damp_grid = damping[None, :, None]
    new_real = system_term[1] + ladder[1] - energy_grid * imag_in - damp_grid * real_in
    new_imag = -system_term[0] - ladder[0] + energy_grid * real_in - damp_grid * imag_in
    return jnp.stack([new_real, new_imag]).astype(jnp.bfloat16)


def one_hot(shape, hit):
    row = lax.broadcasted_iota(jnp.int32, shape, 0)
    col = lax.broadcasted_iota(jnp.int32, shape, 1)
    return jnp.where(hit(row, col), 1.0, 0.0).astype(jnp.bfloat16)


def product(left, right):
    return jnp.dot(left, right, preferred_element_type=jnp.float32)


def picked(left, right):
    return product(left, right).astype(jnp.bfloat16)


def symmetric_tile(matrix, factor):
    size = matrix.shape[0]
    eye = one_hot((size, size), lambda row, col: row == col)
    turned = lax.dot_general(
        matrix, eye, (((0,), (0,)), ((), ())), preferred_element_type=jnp.float32
    )
    return ((matrix.astype(jnp.float32) + factor * turned) * 0.5).astype(jnp.bfloat16)


def ladder_matrix(ham, coupling, strength, first_state):
    levels = ham.shape[0]
    size = levels * ROWS
    tall = one_hot((size, levels), lambda row, col: row // ROWS == col)
    wide = one_hot((levels, size), lambda row, col: row == col // ROWS)
    ham_all = product(picked(tall, symmetric_tile(ham, 1.0)), wide)
    coupling_all = product(picked(tall, symmetric_tile(coupling, 1.0)), wide)
    states = strength.shape[1]
    row = lax.broadcasted_iota(jnp.int32, (size, states), 0)
    col = lax.broadcasted_iota(jnp.int32, (size, states), 1)
    gain = jnp.sum(
        jnp.where(col == first_state + row % ROWS, strength, 0.0), axis=1, keepdims=True
    )
    row = lax.broadcasted_iota(jnp.int32, (size, size), 0)
    col = lax.broadcasted_iota(jnp.int32, (size, size), 1)
    mixed = ham_all + gain * coupling_all
    return jnp.where(row % ROWS == col % ROWS, mixed, 0.0).astype(jnp.bfloat16)


def system_matrix(system_real, system_imag, sys_index, local):
    states = system_real.shape[0]
    rows = one_hot((local, states), lambda row, col: col == row + local * sys_index)
    real = picked(rows, symmetric_tile(system_real, 1.0))
    imag = picked(rows, symmetric_tile(system_imag, -1.0))

    def place(part):
        def hit(row, col):
            block = col // local
            side = jnp.where(block < 2, sys_index, 1 - sys_index)
            return (block % 2 == part) & (row == col % local + local * side)

        return one_hot((states, 2 * states), hit)

    to_real, to_imag = place(0), place(1)
    upper = product(imag, to_real) + product(real, to_imag)
    lower = product(imag, to_imag) - product(real, to_real)
    return jnp.concatenate([upper, lower], axis=0).astype(jnp.bfloat16)


def section_kernel(
    count,
    dens,
    system_real,
    system_imag,
    left_ham,
    left_coupling,
    right_ham,
    right_coupling,
    left_strength,
    right_strength,
    left_damping,
    right_damping,
    energies,
    other,
    left_out,
    mine,
    level,
    taken,
    given,
    rest,
    left_mat,
    right_mat,
    sys_mat,
    fwd_send,
    fwd_recv,
    ret_send,
    ret_recv,
    sys_send,
    sys_recv,
    level_sem,
    mine_sem,
):
    me = lax.axis_index("rc")
    sys_index = lax.axis_index("sys")
    _, halves, half, local, columns = dens.shape
    levels = 2 * half
    row_blocks, lane_blocks = local // ROWS, columns // LANES
    chunks = half // STEP
    odd = lax.rem(me, 2)
    partner = me + 1 - 2 * odd
    shared = (halves - 1) * (1 - odd)

    def task(rank):
        part = rank // (row_blocks * lane_blocks)
        row = lax.rem(rank // lane_blocks, row_blocks) * ROWS
        lane = lax.rem(rank, lane_blocks) * LANES
        return part, pl.ds(pl.multiple_of(row, ROWS), ROWS), pl.ds(pl.multiple_of(lane, LANES), LANES)

    def peer(turn):
        side = count // 2
        other_side = lax.rem(turn, 2)
        return lax.rem(me // side + other_side, 2) * side + lax.rem(me + turn // 2, side)

    def part_of(rank, chunk):
        part, row, lane = task(rank)
        return dens.at[part, :, pl.ds(chunk * STEP, STEP), row, lane]

    def forward(chunk, rank, owner):
        return pltpu.make_async_remote_copy(
            src_ref=part_of(rank, chunk),
            dst_ref=taken.at[chunk, pl.ds(owner * halves, halves)],
            send_sem=fwd_send.at[chunk, rank],
            recv_sem=fwd_recv.at[chunk, owner],
            device_id={"rc": rank},
            device_id_type=pl.DeviceIdType.MESH,
        )

    def forward_own(chunk):
        return pltpu.make_async_copy(
            part_of(me, chunk), taken.at[chunk, pl.ds(me * halves, halves)], fwd_recv.at[chunk, me]
        )

    def landing(rank, chunk):
        part, row, lane = task(rank)
        return left_out.at[1 - part, :, pl.ds(chunk * STEP, STEP), row, lane]

    def giveback(chunk, rank, worker):
        return pltpu.make_async_remote_copy(
            src_ref=given.at[chunk, pl.ds(rank * halves, halves)],
            dst_ref=landing(worker, chunk),
            send_sem=ret_send.at[chunk, rank],
            recv_sem=ret_recv.at[chunk, worker],
            device_id={"rc": rank},
            device_id_type=pl.DeviceIdType.MESH,
        )

    def giveback_own(chunk):
        return pltpu.make_async_copy(
            given.at[chunk, pl.ds(me * halves, halves)], landing(me, chunk), ret_recv.at[chunk, me]
        )

    def swap(index):
        return pltpu.make_async_remote_copy(
            src_ref=dens.at[:, index],
            dst_ref=other.at[:, index],
            send_sem=sys_send.at[index],
            recv_sem=sys_recv.at[index],
            device_id={"sys": 1 - sys_index},
            device_id_type=pl.DeviceIdType.MESH,
        )

    barrier = pltpu.get_barrier_semaphore()

    @pl.loop(1, count)
    def _(offset):
        pl.semaphore_signal(
            barrier, inc=1, device_id={"rc": peer(offset)}, device_id_type=pl.DeviceIdType.MESH
        )

    pl.semaphore_signal(
        barrier, inc=1, device_id={"sys": 1 - sys_index}, device_id_type=pl.DeviceIdType.MESH
    )
    pl.semaphore_wait(barrier, count)

    level_copy = pltpu.make_async_remote_copy(
        src_ref=dens.at[:, shared],
        dst_ref=level.at[:, odd],
        send_sem=level_sem.at[0],
        recv_sem=level_sem.at[1],
        device_id={"rc": partner},
        device_id_type=pl.DeviceIdType.MESH,
    )
    level_copy.start()
    level_own = pltpu.make_async_copy(dens.at[:, shared], level.at[:, odd], level_sem.at[2])
    level_own.start()
    mine_copy = pltpu.make_async_copy(dens, mine, mine_sem)
    mine_copy.start()

    @pl.loop(0, chunks)
    def _(chunk):
        forward_own(chunk).start()

        @pl.loop(1, count)
        def _(offset):
            forward(chunk, peer(offset), me).start()

        swap(chunk).start()

    @pl.loop(chunks, halves)
    def _(index):
        swap(index).start()

    my_part = me // (row_blocks * lane_blocks)
    my_row = lax.rem(me // lane_blocks, row_blocks) * ROWS
    left_mat[...] = ladder_matrix(
        left_ham[...], left_coupling[...], left_strength[...], sys_index * local + my_row
    )
    for block in range(row_blocks):
        right_mat[block] = ladder_matrix(
            right_ham[...],
            right_coupling[...],
            right_strength[...],
            sys_index * local + block * ROWS,
        )
    sys_mat[...] = system_matrix(system_real[...], system_imag[...], sys_index, local)

    mine_copy.wait()
    level_own.wait()
    level_copy.wait()
    full_levels = halves // 2

    @pl.loop(0, 2)
    def _(part):
        sign = jnp.where(part == 1, 1.0, -1.0)
        for block in range(row_blocks):
            row = pl.ds(block * ROWS, ROWS)

            @pl.loop(0, full_levels)
            def _(number):
                first = odd + 2 * number
                held = mine[part, pl.ds(first, 2), :, row, :].reshape(levels * ROWS, columns)
                term = product(right_mat[block], held) * sign
                rest[1 - part, pl.ds(first, 2), :, row, :] = term.reshape(2, half, ROWS, columns)

            held = level[part, :, :, row, :].reshape(levels * ROWS, columns)
            rows = pl.ds(pl.multiple_of(odd * half * ROWS, half * ROWS), half * ROWS)
            term = product(right_mat[block, rows, :], held) * sign
            rest[1 - part, shared, :, row, :] = term.reshape(half, ROWS, columns)

    def system_rows(index):
        swap(index).wait_recv()

        @pl.loop(0, half)
        def _(at):
            pair = (me * halves + index) * half + at
            damping = 0.5 * (left_damping[pair // levels] + right_damping[lax.rem(pair, levels)])
            real, imag = mine[0, index, at], mine[1, index, at]
            held = jnp.concatenate([real, imag, other[0, index, at], other[1, index, at]], axis=0)
            term = product(sys_mat[...], held)
            real, imag = real.astype(jnp.float32), imag.astype(jnp.float32)
            energy = energies[...]
            new_real = term[:local] + rest[0, index, at] - energy * imag - damping * real
            new_imag = term[local:] + rest[1, index, at] + energy * real - damping * imag
            other[0, index, at] = new_real.astype(jnp.bfloat16)
            other[1, index, at] = new_imag.astype(jnp.bfloat16)

    my_sign = jnp.where(my_part == 1, 1.0, -1.0)

    @pl.loop(0, chunks)
    def _(chunk):
        forward_own(chunk).wait()

        @pl.loop(1, count)
        def _(offset):
            forward(chunk, me, peer(offset)).wait_recv()

        for side in range(2):
            held = jnp.concatenate(
                [
                    jnp.concatenate(
                        [taken[chunk, 2 * number + side, at] for number in range(levels)], axis=0
                    )
                    for at in range(STEP)
                ],
                axis=1,
            )
            term = (product(left_mat[...], held) * my_sign).astype(jnp.bfloat16)
            for at in range(STEP):
                for number in range(levels):
                    given[chunk, 2 * number + side, at] = term[
                        number * ROWS : (number + 1) * ROWS, at * LANES : (at + 1) * LANES
                    ]
        giveback_own(chunk).start()

        @pl.loop(1, count)
        def _(offset):
            giveback(chunk, peer(offset), me).start()

        first = chunk * halves // (chunks - 1)
        last = jnp.minimum((chunk + 1) * halves // (chunks - 1), halves)

        @pl.loop(first, last)
        def _(index):
            system_rows(index)

    @pl.loop(0, halves)
    def _(index):
        swap(index).wait_send()

    @pl.loop(0, chunks)
    def _(chunk):
        giveback_own(chunk).wait()

        @pl.loop(1, count)
        def _(offset):
            rank = peer(offset)
            forward(chunk, rank, me).wait_send()
            giveback(chunk, rank, me).wait_send()
            giveback(chunk, me, rank).wait_recv()


def add_kernel(rest, left, total, staged, sems):
    _, halves = rest.shape[:2]

    def out(part, index):
        return pltpu.make_async_copy(
            staged.at[part, index], total.at[part, index], sems.at[part, index]
        )

    for part in range(2):

        @pl.loop(0, halves)
        def _(index):
            summed = rest[part, index].astype(jnp.float32) + left[part, index].astype(jnp.float32)
            staged[part, index] = summed.astype(jnp.bfloat16)
            out(part, index).start()

    for part in range(2):

        @pl.loop(0, halves)
        def _(index):
            out(part, index).wait()


def exchanged(
    density,
    system_real,
    system_imag,
    left_ham,
    left_coupling,
    right_ham,
    right_coupling,
    left_strength,
    right_strength,
    left_damping,
    right_damping,
    energies,
):
    count = lax.axis_size("rc")
    levels = left_ham.shape[0]
    half = levels // 2
    _, local, pairs, columns = density.shape
    halves = pairs // half
    chunks = half // STEP
    size = levels * ROWS
    row_blocks = local // ROWS
    dens = jnp.transpose(density, (0, 2, 1, 3)).reshape(2, halves, half, local, columns)
    whole = pl.BlockSpec(memory_space=pltpu.VMEM)
    scalars = pl.BlockSpec(memory_space=pltpu.SMEM)
    anywhere = pl.BlockSpec(memory_space=pl.ANY)
    slab = jax.ShapeDtypeStruct(dens.shape, jnp.bfloat16)
    rest, left = pl.pallas_call(
        functools.partial(section_kernel, count),
        out_shape=[pltpu.VMEM(dens.shape, jnp.bfloat16)] * 2,
        in_specs=[anywhere] + [whole] * 8 + [scalars] * 2 + [whole],
        out_specs=[whole, whole],
        scratch_shapes=[
            pltpu.VMEM(dens.shape, jnp.bfloat16),
            pltpu.VMEM((2, 2, half, local, columns), jnp.bfloat16),
            pltpu.VMEM((chunks, count * halves, STEP, ROWS, LANES), jnp.bfloat16),
            pltpu.VMEM((chunks, count * halves, STEP, ROWS, LANES), jnp.bfloat16),
            pltpu.VMEM(dens.shape, jnp.float32),
            pltpu.VMEM((size, size), jnp.bfloat16),
            pltpu.VMEM((row_blocks, size, size), jnp.bfloat16),
            pltpu.VMEM((2 * local, 4 * local), jnp.bfloat16),
            pltpu.SemaphoreType.DMA((chunks, count)),
            pltpu.SemaphoreType.DMA((chunks, count)),
            pltpu.SemaphoreType.DMA((chunks, count)),
            pltpu.SemaphoreType.DMA((chunks, count)),
            pltpu.SemaphoreType.DMA((halves,)),
            pltpu.SemaphoreType.DMA((halves,)),
            pltpu.SemaphoreType.DMA((3,)),
            pltpu.SemaphoreType.DMA,
        ],
        compiler_params=pltpu.CompilerParams(
            collective_id=0, has_side_effects=True, vmem_limit_bytes=46 * 2**20
        ),
        cost_estimate=pl.CostEstimate(
            flops=10 * 10**9, bytes_accessed=5 * dens.size * 2, transcendentals=0
        ),
    )(
        dens,
        system_real,
        system_imag,
        left_ham,
        left_coupling,
        right_ham,
        right_coupling,
        left_strength[None, :],
        right_strength[None, :],
        left_damping,
        right_damping,
        energies[None, :],
    )
    total = pl.pallas_call(
        add_kernel,
        out_shape=slab,
        in_specs=[whole, whole],
        out_specs=anywhere,
        scratch_shapes=[
            pltpu.VMEM(dens.shape, jnp.bfloat16),
            pltpu.SemaphoreType.DMA((2, halves)),
        ],
        compiler_params=pltpu.CompilerParams(vmem_limit_bytes=32 * 2**20),
        cost_estimate=pl.CostEstimate(
            flops=dens.size, bytes_accessed=dens.size * 2, transcendentals=0
        ),
    )(rest, left)
    return jnp.transpose(total.reshape(2, pairs, local, columns), (0, 2, 1, 3))


def fits(mesh, shapes):
    count, sides = mesh.shape["rc"], mesh.shape["sys"]
    _, states, pairs, columns = shapes[0]
    levels = shapes[3][0]
    if sides != 2 or levels % 2 or pairs % count or states % (2 * ROWS) or columns % LANES:
        return False
    half, local_pairs = levels // 2, pairs // count
    tasks = 2 * (states // (2 * ROWS)) * (columns // LANES)
    return (
        tasks == count
        and half % STEP == 0
        and local_pairs % half == 0
        and local_pairs // half % 2 == 1
        and local_pairs // half >= half // STEP > 1
    )


def solution(mesh):
    placed = (P(None, "sys", "rc", None), P(), P(), P(), P(), P(), P(), P(), P(), P(), P(), P())

    def run(*arrays):
        body = exchanged if fits(mesh, [array.shape for array in arrays]) else shards
        return jax.shard_map(
            body, mesh=mesh, in_specs=placed, out_specs=P(None, "sys", "rc", None), check_vma=False
        )(*arrays)

    return run
```

```python
import functools
import math

import jax
import jax.numpy as jnp
from jax import lax
from jax.experimental import pallas as pl
from jax.experimental.pallas import tpu as pltpu
from jax.sharding import PartitionSpec as P

ROWS = 16
LANES = 128


def symmetric(matrix, factor):
    widened = matrix.astype(jnp.float32)
    return ((widened + factor * widened.T) * 0.5).astype(jnp.bfloat16)


def ladder_local(regrouped, left_ops, right_ops, left_gain, right_gain, levels):
    item_count, group_count, all_pairs, column_count = regrouped.shape
    widened = regrouped.reshape(item_count, group_count, levels, levels * column_count)
    left_all = jnp.einsum("xa,ksam->ksxm", left_ops, widened, preferred_element_type=jnp.float32)
    left_term = left_all[:, :, :levels] + left_gain[None, :, None, None] * left_all[:, :, levels:]
    deepened = regrouped.reshape(item_count, group_count, levels, levels, column_count)
    right_all = jnp.einsum(
        "yb,ksabc->ksayc", right_ops, deepened, preferred_element_type=jnp.float32
    )
    right_term = (
        right_all[:, :, :, :levels]
        + right_gain[None, :, None, None, None] * right_all[:, :, :, levels:]
    )
    summed = left_term.reshape(
        item_count, group_count, all_pairs, column_count
    ) + right_term.reshape(item_count, group_count, all_pairs, column_count)
    return summed.astype(jnp.bfloat16)


def shards(
    density,
    system_real,
    system_imag,
    left_ham,
    left_coupling,
    right_ham,
    right_coupling,
    left_strength,
    right_strength,
    left_damping,
    right_damping,
    energies,
):
    herm_real = symmetric(system_real, 1.0)
    herm_imag = symmetric(system_imag, -1.0)
    levels = left_ham.shape[0]
    left_ops = jnp.concatenate([symmetric(left_ham, 1.0), symmetric(left_coupling, 1.0)], axis=0)
    right_ops = jnp.concatenate([symmetric(right_ham, 1.0), symmetric(right_coupling, 1.0)], axis=0)
    state_count = density.shape[1]
    pair_count = density.shape[2]
    column_total = density.shape[3]
    first_state = lax.axis_index("sys") * state_count
    left_gain = lax.dynamic_slice_in_dim(left_strength, first_state, state_count)
    right_gain = lax.dynamic_slice_in_dim(right_strength, first_state, state_count)
    regrouped = lax.all_to_all(density, "sys", split_axis=3, concat_axis=1, tiled=True)
    flattened = regrouped.reshape(2, regrouped.shape[1], -1)
    real_part = jnp.dot(herm_real, flattened[0], preferred_element_type=jnp.float32) - jnp.dot(
        herm_imag, flattened[1], preferred_element_type=jnp.float32
    )
    imag_part = jnp.dot(herm_real, flattened[1], preferred_element_type=jnp.float32) + jnp.dot(
        herm_imag, flattened[0], preferred_element_type=jnp.float32
    )
    product = jnp.stack([real_part, imag_part]).astype(jnp.bfloat16).reshape(regrouped.shape)
    system_rows = lax.all_to_all(product, "sys", split_axis=1, concat_axis=3, tiled=True)
    rc_count = lax.axis_size("rc")
    col_groups = rc_count // math.gcd(state_count, rc_count)
    per_device = state_count * col_groups // rc_count
    group_width = column_total // col_groups
    combined = jnp.moveaxis(
        density.reshape(2, state_count, pair_count, col_groups, group_width), 3, 2
    )
    combined = combined.reshape(2, state_count * col_groups, pair_count, group_width)
    combo_index = lax.axis_index("rc") * per_device + jnp.arange(per_device, dtype=jnp.int32)
    state_pick = (
        (combo_index // col_groups)[:, None] == jnp.arange(state_count, dtype=jnp.int32)[None, :]
    ).astype(jnp.float32)
    combo_left = jnp.sum(state_pick * left_gain[None, :], axis=1)
    combo_right = jnp.sum(state_pick * right_gain[None, :], axis=1)
    summed = ladder_local(
        lax.all_to_all(combined, "rc", split_axis=1, concat_axis=2, tiled=True),
        left_ops,
        right_ops,
        combo_left,
        combo_right,
        levels,
    )
    returned = lax.all_to_all(summed, "rc", split_axis=2, concat_axis=1, tiled=True)
    returned = returned.reshape(2, state_count, col_groups, pair_count, group_width)
    ladder_rows = jnp.moveaxis(returned, 2, 3).reshape(2, state_count, pair_count, column_total)
    pair_index = lax.axis_index("rc") * pair_count + jnp.arange(pair_count, dtype=jnp.int32)
    level_index = jnp.arange(levels, dtype=jnp.int32)
    left_pick = (pair_index[:, None] // levels == level_index[None, :]).astype(jnp.float32)
    right_pick = (pair_index[:, None] % levels == level_index[None, :]).astype(jnp.float32)
    damping = 0.5 * (
        jnp.sum(left_pick * left_damping[None, :], axis=1)
        + jnp.sum(right_pick * right_damping[None, :], axis=1)
    )
    system_term = system_rows.astype(jnp.float32)
    ladder = ladder_rows.astype(jnp.float32)
    real_in = density[0].astype(jnp.float32)
    imag_in = density[1].astype(jnp.float32)
    energy_grid = energies[None, None, :]
    damp_grid = damping[None, :, None]
    new_real = system_term[1] + ladder[1] - energy_grid * imag_in - damp_grid * real_in
    new_imag = -system_term[0] - ladder[0] + energy_grid * real_in - damp_grid * imag_in
    return jnp.stack([new_real, new_imag]).astype(jnp.bfloat16)


def one_hot(shape, hit):
    row = lax.broadcasted_iota(jnp.int32, shape, 0)
    col = lax.broadcasted_iota(jnp.int32, shape, 1)
    return jnp.where(hit(row, col), 1.0, 0.0).astype(jnp.bfloat16)


def product(left, right):
    return jnp.dot(left, right, preferred_element_type=jnp.float32)


def picked(left, right):
    return product(left, right).astype(jnp.bfloat16)


def symmetric_tile(matrix, factor):
    size = matrix.shape[0]
    eye = one_hot((size, size), lambda row, col: row == col)
    turned = lax.dot_general(
        matrix, eye, (((0,), (0,)), ((), ())), preferred_element_type=jnp.float32
    )
    return ((matrix.astype(jnp.float32) + factor * turned) * 0.5).astype(jnp.bfloat16)


def ladder_matrix(ham, coupling, strength, first_state):
    levels = ham.shape[0]
    size = levels * ROWS
    tall = one_hot((size, levels), lambda row, col: row // ROWS == col)
    wide = one_hot((levels, size), lambda row, col: row == col // ROWS)
    ham_all = product(picked(tall, symmetric_tile(ham, 1.0)), wide)
    coupling_all = product(picked(tall, symmetric_tile(coupling, 1.0)), wide)
    states = strength.shape[1]
    row = lax.broadcasted_iota(jnp.int32, (size, states), 0)
    col = lax.broadcasted_iota(jnp.int32, (size, states), 1)
    gain = jnp.sum(
        jnp.where(col == first_state + row % ROWS, strength, 0.0), axis=1, keepdims=True
    )
    row = lax.broadcasted_iota(jnp.int32, (size, size), 0)
    col = lax.broadcasted_iota(jnp.int32, (size, size), 1)
    mixed = ham_all + gain * coupling_all
    return jnp.where(row % ROWS == col % ROWS, mixed, 0.0).astype(jnp.bfloat16)


def system_matrix(system_real, system_imag, sys_index, local):
    states = system_real.shape[0]
    rows = one_hot((local, states), lambda row, col: col == row + local * sys_index)
    real = picked(rows, symmetric_tile(system_real, 1.0))
    imag = picked(rows, symmetric_tile(system_imag, -1.0))

    def place(part):
        def hit(row, col):
            block = col // local
            side = jnp.where(block < 2, sys_index, 1 - sys_index)
            return (block % 2 == part) & (row == col % local + local * side)

        return one_hot((states, 2 * states), hit)

    to_real, to_imag = place(0), place(1)
    upper = product(imag, to_real) + product(real, to_imag)
    lower = product(imag, to_imag) - product(real, to_real)
    return jnp.concatenate([upper, lower], axis=0).astype(jnp.bfloat16)


def section_kernel(
    count,
    dens,
    system_real,
    system_imag,
    left_ham,
    left_coupling,
    right_ham,
    right_coupling,
    left_strength,
    right_strength,
    left_damping,
    right_damping,
    energies,
    other,
    left_out,
    mine,
    level,
    taken,
    given,
    rest,
    left_mat,
    right_mat,
    sys_mat,
    fwd_send,
    fwd_recv,
    ret_send,
    ret_recv,
    sys_send,
    sys_recv,
    level_sem,
    mine_sem,
):
    me = lax.axis_index("rc")
    sys_index = lax.axis_index("sys")
    _, halves, half, local, columns = dens.shape
    levels = 2 * half
    row_blocks = local // ROWS
    parts = count // (2 * row_blocks)
    chunks = half // parts
    odd = lax.rem(me, 2)
    partner = me + 1 - 2 * odd
    shared = (halves - 1) * (1 - odd)

    def task(rank, chunk):
        part = rank // (row_blocks * parts)
        row = lax.rem(rank // parts, row_blocks) * ROWS
        return part, lax.rem(rank, parts) * chunks + chunk, pl.ds(pl.multiple_of(row, ROWS), ROWS)

    def peer(turn):
        side = count // 2
        other_side = lax.rem(turn, 2)
        return lax.rem(me // side + other_side, 2) * side + lax.rem(me + turn // 2, side)

    def part_of(rank, chunk):
        part, at, row = task(rank, chunk)
        return dens.at[part, :, at, row, :]

    def forward(chunk, rank, owner):
        return pltpu.make_async_remote_copy(
            src_ref=part_of(rank, chunk),
            dst_ref=taken.at[chunk, pl.ds(owner * halves, halves)],
            send_sem=fwd_send.at[chunk, rank],
            recv_sem=fwd_recv.at[chunk, owner],
            device_id={"rc": rank},
            device_id_type=pl.DeviceIdType.MESH,
        )

    def forward_own(chunk):
        return pltpu.make_async_copy(
            part_of(me, chunk), taken.at[chunk, pl.ds(me * halves, halves)], fwd_recv.at[chunk, me]
        )

    def landing(rank, chunk):
        part, at, row = task(rank, chunk)
        return left_out.at[1 - part, :, at, row, :]

    def giveback(chunk, rank, worker):
        return pltpu.make_async_remote_copy(
            src_ref=given.at[chunk, pl.ds(rank * halves, halves)],
            dst_ref=landing(worker, chunk),
            send_sem=ret_send.at[chunk, rank],
            recv_sem=ret_recv.at[chunk, worker],
            device_id={"rc": rank},
            device_id_type=pl.DeviceIdType.MESH,
        )

    def giveback_own(chunk):
        return pltpu.make_async_copy(
            given.at[chunk, pl.ds(me * halves, halves)], landing(me, chunk), ret_recv.at[chunk, me]
        )

    def swap(index):
        return pltpu.make_async_remote_copy(
            src_ref=dens.at[:, index],
            dst_ref=other.at[:, index],
            send_sem=sys_send.at[index],
            recv_sem=sys_recv.at[index],
            device_id={"sys": 1 - sys_index},
            device_id_type=pl.DeviceIdType.MESH,
        )

    barrier = pltpu.get_barrier_semaphore()

    @pl.loop(1, count)
    def _(offset):
        pl.semaphore_signal(
            barrier, inc=1, device_id={"rc": peer(offset)}, device_id_type=pl.DeviceIdType.MESH
        )

    pl.semaphore_signal(
        barrier, inc=1, device_id={"sys": 1 - sys_index}, device_id_type=pl.DeviceIdType.MESH
    )
    pl.semaphore_wait(barrier, count)

    level_copy = pltpu.make_async_remote_copy(
        src_ref=dens.at[:, shared],
        dst_ref=level.at[:, odd],
        send_sem=level_sem.at[0],
        recv_sem=level_sem.at[1],
        device_id={"rc": partner},
        device_id_type=pl.DeviceIdType.MESH,
    )
    level_copy.start()
    level_own = pltpu.make_async_copy(dens.at[:, shared], level.at[:, odd], level_sem.at[2])
    level_own.start()
    mine_copy = pltpu.make_async_copy(dens, mine, mine_sem)
    mine_copy.start()

    @pl.loop(0, chunks)
    def _(chunk):
        forward_own(chunk).start()

        @pl.loop(1, count)
        def _(offset):
            forward(chunk, peer(offset), me).start()

        swap(chunk).start()

    @pl.loop(chunks, halves)
    def _(index):
        swap(index).start()

    my_part = me // (row_blocks * parts)
    my_row = lax.rem(me // parts, row_blocks) * ROWS
    left_mat[...] = ladder_matrix(
        left_ham[...], left_coupling[...], left_strength[...], sys_index * local + my_row
    )
    for block in range(row_blocks):
        right_mat[block] = ladder_matrix(
            right_ham[...],
            right_coupling[...],
            right_strength[...],
            sys_index * local + block * ROWS,
        )
    sys_mat[...] = system_matrix(system_real[...], system_imag[...], sys_index, local)

    mine_copy.wait()
    level_own.wait()
    level_copy.wait()
    full_levels = halves // 2

    @pl.loop(0, 2)
    def _(part):
        sign = jnp.where(part == 1, 1.0, -1.0)
        for block in range(row_blocks):
            row = pl.ds(block * ROWS, ROWS)

            @pl.loop(0, full_levels)
            def _(number):
                first = odd + 2 * number
                held = mine[part, pl.ds(first, 2), :, row, :].reshape(levels * ROWS, columns)
                term = product(right_mat[block], held) * sign
                rest[1 - part, pl.ds(first, 2), :, row, :] = term.reshape(2, half, ROWS, columns)

            held = level[part, :, :, row, :].reshape(levels * ROWS, columns)
            rows = pl.ds(pl.multiple_of(odd * half * ROWS, half * ROWS), half * ROWS)
            term = product(right_mat[block, rows, :], held) * sign
            rest[1 - part, shared, :, row, :] = term.reshape(half, ROWS, columns)

    def system_rows(index):
        swap(index).wait_recv()

        @pl.loop(0, half)
        def _(at):
            pair = (me * halves + index) * half + at
            damping = 0.5 * (left_damping[pair // levels] + right_damping[lax.rem(pair, levels)])
            real, imag = mine[0, index, at], mine[1, index, at]
            held = jnp.concatenate([real, imag, other[0, index, at], other[1, index, at]], axis=0)
            term = product(sys_mat[...], held)
            real, imag = real.astype(jnp.float32), imag.astype(jnp.float32)
            energy = energies[...]
            new_real = term[:local] + rest[0, index, at] - energy * imag - damping * real
            new_imag = term[local:] + rest[1, index, at] + energy * real - damping * imag
            other[0, index, at] = new_real.astype(jnp.bfloat16)
            other[1, index, at] = new_imag.astype(jnp.bfloat16)

    my_sign = jnp.where(my_part == 1, 1.0, -1.0)

    @pl.loop(0, chunks)
    def _(chunk):
        forward_own(chunk).wait()

        @pl.loop(1, count)
        def _(offset):
            forward(chunk, me, peer(offset)).wait_recv()

        for side in range(2):
            held = jnp.concatenate(
                [taken[chunk, 2 * number + side] for number in range(levels)], axis=0
            )
            term = (product(left_mat[...], held) * my_sign).astype(jnp.bfloat16)
            for number in range(levels):
                given[chunk, 2 * number + side] = term[number * ROWS : (number + 1) * ROWS]
        giveback_own(chunk).start()

        @pl.loop(1, count)
        def _(offset):
            giveback(chunk, peer(offset), me).start()

        first = chunk * halves // (chunks - 1)
        last = jnp.minimum((chunk + 1) * halves // (chunks - 1), halves)

        @pl.loop(first, last)
        def _(index):
            system_rows(index)

    @pl.loop(0, halves)
    def _(index):
        swap(index).wait_send()

    @pl.loop(0, chunks)
    def _(chunk):
        giveback_own(chunk).wait()

        @pl.loop(1, count)
        def _(offset):
            rank = peer(offset)
            forward(chunk, rank, me).wait_send()
            giveback(chunk, rank, me).wait_send()
            giveback(chunk, me, rank).wait_recv()


def add_kernel(rest, left, total, staged, sems):
    _, halves = rest.shape[:2]

    def out(part, index):
        return pltpu.make_async_copy(
            staged.at[part, index], total.at[part, index], sems.at[part, index]
        )

    for part in range(2):

        @pl.loop(0, halves)
        def _(index):
            summed = rest[part, index].astype(jnp.float32) + left[part, index].astype(jnp.float32)
            staged[part, index] = summed.astype(jnp.bfloat16)
            out(part, index).start()

    for part in range(2):

        @pl.loop(0, halves)
        def _(index):
            out(part, index).wait()


def exchanged(
    density,
    system_real,
    system_imag,
    left_ham,
    left_coupling,
    right_ham,
    right_coupling,
    left_strength,
    right_strength,
    left_damping,
    right_damping,
    energies,
):
    count = lax.axis_size("rc")
    levels = left_ham.shape[0]
    half = levels // 2
    _, local, pairs, columns = density.shape
    halves = pairs // half
    size = levels * ROWS
    row_blocks = local // ROWS
    chunks = half * 2 * row_blocks // count
    dens = jnp.transpose(density, (0, 2, 1, 3)).reshape(2, halves, half, local, columns)
    whole = pl.BlockSpec(memory_space=pltpu.VMEM)
    scalars = pl.BlockSpec(memory_space=pltpu.SMEM)
    anywhere = pl.BlockSpec(memory_space=pl.ANY)
    slab = jax.ShapeDtypeStruct(dens.shape, jnp.bfloat16)
    rest, left = pl.pallas_call(
        functools.partial(section_kernel, count),
        out_shape=[pltpu.VMEM(dens.shape, jnp.bfloat16)] * 2,
        in_specs=[anywhere] + [whole] * 8 + [scalars] * 2 + [whole],
        out_specs=[whole, whole],
        scratch_shapes=[
            pltpu.VMEM(dens.shape, jnp.bfloat16),
            pltpu.VMEM((2, 2, half, local, columns), jnp.bfloat16),
            pltpu.VMEM((chunks, count * halves, ROWS, columns), jnp.bfloat16),
            pltpu.VMEM((chunks, count * halves, ROWS, columns), jnp.bfloat16),
            pltpu.VMEM(dens.shape, jnp.float32),
            pltpu.VMEM((size, size), jnp.bfloat16),
            pltpu.VMEM((row_blocks, size, size), jnp.bfloat16),
            pltpu.VMEM((2 * local, 4 * local), jnp.bfloat16),
            pltpu.SemaphoreType.DMA((chunks, count)),
            pltpu.SemaphoreType.DMA((chunks, count)),
            pltpu.SemaphoreType.DMA((chunks, count)),
            pltpu.SemaphoreType.DMA((chunks, count)),
            pltpu.SemaphoreType.DMA((halves,)),
            pltpu.SemaphoreType.DMA((halves,)),
            pltpu.SemaphoreType.DMA((3,)),
            pltpu.SemaphoreType.DMA,
        ],
        compiler_params=pltpu.CompilerParams(
            collective_id=0, has_side_effects=True, vmem_limit_bytes=46 * 2**20
        ),
        cost_estimate=pl.CostEstimate(
            flops=10 * 10**9, bytes_accessed=5 * dens.size * 2, transcendentals=0
        ),
    )(
        dens,
        system_real,
        system_imag,
        left_ham,
        left_coupling,
        right_ham,
        right_coupling,
        left_strength[None, :],
        right_strength[None, :],
        left_damping,
        right_damping,
        energies[None, :],
    )
    total = pl.pallas_call(
        add_kernel,
        out_shape=slab,
        in_specs=[whole, whole],
        out_specs=anywhere,
        scratch_shapes=[
            pltpu.VMEM(dens.shape, jnp.bfloat16),
            pltpu.SemaphoreType.DMA((2, halves)),
        ],
        compiler_params=pltpu.CompilerParams(vmem_limit_bytes=32 * 2**20),
        cost_estimate=pl.CostEstimate(
            flops=dens.size, bytes_accessed=dens.size * 2, transcendentals=0
        ),
    )(rest, left)
    return jnp.transpose(total.reshape(2, pairs, local, columns), (0, 2, 1, 3))


def fits(mesh, shapes):
    count, sides = mesh.shape["rc"], mesh.shape["sys"]
    _, states, pairs, columns = shapes[0]
    levels = shapes[3][0]
    if sides != 2 or levels % 2 or pairs % count or states % (2 * ROWS) or columns % LANES:
        return False
    half, local_pairs = levels // 2, pairs // count
    row_parts = 2 * (states // (2 * ROWS))
    if count % row_parts or half % (count // row_parts) or local_pairs % half:
        return False
    halves, chunks = local_pairs // half, half * row_parts // count
    return halves % 2 == 1 and halves >= chunks > 1


def solution(mesh):
    placed = (P(None, "sys", "rc", None), P(), P(), P(), P(), P(), P(), P(), P(), P(), P(), P())

    def run(*arrays):
        body = exchanged if fits(mesh, [array.shape for array in arrays]) else shards
        return jax.shard_map(
            body, mesh=mesh, in_specs=placed, out_specs=P(None, "sys", "rc", None), check_vma=False
        )(*arrays)

    return run
```

```python
import functools
import math

import jax
import jax.numpy as jnp
from jax import lax
from jax.experimental import pallas as pl
from jax.experimental.pallas import tpu as pltpu
from jax.sharding import PartitionSpec as P

ROWS = 16
LANES = 128
AHEAD = 2


def symmetric(matrix, factor):
    widened = matrix.astype(jnp.float32)
    return ((widened + factor * widened.T) * 0.5).astype(jnp.bfloat16)


def ladder_local(regrouped, left_ops, right_ops, left_gain, right_gain, levels):
    item_count, group_count, all_pairs, column_count = regrouped.shape
    widened = regrouped.reshape(item_count, group_count, levels, levels * column_count)
    left_all = jnp.einsum("xa,ksam->ksxm", left_ops, widened, preferred_element_type=jnp.float32)
    left_term = left_all[:, :, :levels] + left_gain[None, :, None, None] * left_all[:, :, levels:]
    deepened = regrouped.reshape(item_count, group_count, levels, levels, column_count)
    right_all = jnp.einsum(
        "yb,ksabc->ksayc", right_ops, deepened, preferred_element_type=jnp.float32
    )
    right_term = (
        right_all[:, :, :, :levels]
        + right_gain[None, :, None, None, None] * right_all[:, :, :, levels:]
    )
    summed = left_term.reshape(
        item_count, group_count, all_pairs, column_count
    ) + right_term.reshape(item_count, group_count, all_pairs, column_count)
    return summed.astype(jnp.bfloat16)


def shards(
    density,
    system_real,
    system_imag,
    left_ham,
    left_coupling,
    right_ham,
    right_coupling,
    left_strength,
    right_strength,
    left_damping,
    right_damping,
    energies,
):
    herm_real = symmetric(system_real, 1.0)
    herm_imag = symmetric(system_imag, -1.0)
    levels = left_ham.shape[0]
    left_ops = jnp.concatenate([symmetric(left_ham, 1.0), symmetric(left_coupling, 1.0)], axis=0)
    right_ops = jnp.concatenate([symmetric(right_ham, 1.0), symmetric(right_coupling, 1.0)], axis=0)
    state_count = density.shape[1]
    pair_count = density.shape[2]
    column_total = density.shape[3]
    first_state = lax.axis_index("sys") * state_count
    left_gain = lax.dynamic_slice_in_dim(left_strength, first_state, state_count)
    right_gain = lax.dynamic_slice_in_dim(right_strength, first_state, state_count)
    regrouped = lax.all_to_all(density, "sys", split_axis=3, concat_axis=1, tiled=True)
    flattened = regrouped.reshape(2, regrouped.shape[1], -1)
    real_part = jnp.dot(herm_real, flattened[0], preferred_element_type=jnp.float32) - jnp.dot(
        herm_imag, flattened[1], preferred_element_type=jnp.float32
    )
    imag_part = jnp.dot(herm_real, flattened[1], preferred_element_type=jnp.float32) + jnp.dot(
        herm_imag, flattened[0], preferred_element_type=jnp.float32
    )
    product = jnp.stack([real_part, imag_part]).astype(jnp.bfloat16).reshape(regrouped.shape)
    system_rows = lax.all_to_all(product, "sys", split_axis=1, concat_axis=3, tiled=True)
    rc_count = lax.axis_size("rc")
    col_groups = rc_count // math.gcd(state_count, rc_count)
    per_device = state_count * col_groups // rc_count
    group_width = column_total // col_groups
    combined = jnp.moveaxis(
        density.reshape(2, state_count, pair_count, col_groups, group_width), 3, 2
    )
    combined = combined.reshape(2, state_count * col_groups, pair_count, group_width)
    combo_index = lax.axis_index("rc") * per_device + jnp.arange(per_device, dtype=jnp.int32)
    state_pick = (
        (combo_index // col_groups)[:, None] == jnp.arange(state_count, dtype=jnp.int32)[None, :]
    ).astype(jnp.float32)
    combo_left = jnp.sum(state_pick * left_gain[None, :], axis=1)
    combo_right = jnp.sum(state_pick * right_gain[None, :], axis=1)
    summed = ladder_local(
        lax.all_to_all(combined, "rc", split_axis=1, concat_axis=2, tiled=True),
        left_ops,
        right_ops,
        combo_left,
        combo_right,
        levels,
    )
    returned = lax.all_to_all(summed, "rc", split_axis=2, concat_axis=1, tiled=True)
    returned = returned.reshape(2, state_count, col_groups, pair_count, group_width)
    ladder_rows = jnp.moveaxis(returned, 2, 3).reshape(2, state_count, pair_count, column_total)
    pair_index = lax.axis_index("rc") * pair_count + jnp.arange(pair_count, dtype=jnp.int32)
    level_index = jnp.arange(levels, dtype=jnp.int32)
    left_pick = (pair_index[:, None] // levels == level_index[None, :]).astype(jnp.float32)
    right_pick = (pair_index[:, None] % levels == level_index[None, :]).astype(jnp.float32)
    damping = 0.5 * (
        jnp.sum(left_pick * left_damping[None, :], axis=1)
        + jnp.sum(right_pick * right_damping[None, :], axis=1)
    )
    system_term = system_rows.astype(jnp.float32)
    ladder = ladder_rows.astype(jnp.float32)
    real_in = density[0].astype(jnp.float32)
    imag_in = density[1].astype(jnp.float32)
    energy_grid = energies[None, None, :]
    damp_grid = damping[None, :, None]
    new_real = system_term[1] + ladder[1] - energy_grid * imag_in - damp_grid * real_in
    new_imag = -system_term[0] - ladder[0] + energy_grid * real_in - damp_grid * imag_in
    return jnp.stack([new_real, new_imag]).astype(jnp.bfloat16)


def one_hot(shape, hit):
    row = lax.broadcasted_iota(jnp.int32, shape, 0)
    col = lax.broadcasted_iota(jnp.int32, shape, 1)
    return jnp.where(hit(row, col), 1.0, 0.0).astype(jnp.bfloat16)


def product(left, right):
    return jnp.dot(left, right, preferred_element_type=jnp.float32)


def picked(left, right):
    return product(left, right).astype(jnp.bfloat16)


def symmetric_tile(matrix, factor):
    size = matrix.shape[0]
    eye = one_hot((size, size), lambda row, col: row == col)
    turned = lax.dot_general(
        matrix, eye, (((0,), (0,)), ((), ())), preferred_element_type=jnp.float32
    )
    return ((matrix.astype(jnp.float32) + factor * turned) * 0.5).astype(jnp.bfloat16)


def ladder_matrix(ham, coupling, strength, first_state):
    levels = ham.shape[0]
    size = levels * ROWS
    tall = one_hot((size, levels), lambda row, col: row // ROWS == col)
    wide = one_hot((levels, size), lambda row, col: row == col // ROWS)
    ham_all = product(picked(tall, symmetric_tile(ham, 1.0)), wide)
    coupling_all = product(picked(tall, symmetric_tile(coupling, 1.0)), wide)
    states = strength.shape[1]
    row = lax.broadcasted_iota(jnp.int32, (size, states), 0)
    col = lax.broadcasted_iota(jnp.int32, (size, states), 1)
    gain = jnp.sum(
        jnp.where(col == first_state + row % ROWS, strength, 0.0), axis=1, keepdims=True
    )
    row = lax.broadcasted_iota(jnp.int32, (size, size), 0)
    col = lax.broadcasted_iota(jnp.int32, (size, size), 1)
    mixed = ham_all + gain * coupling_all
    return jnp.where(row % ROWS == col % ROWS, mixed, 0.0).astype(jnp.bfloat16)


def system_matrix(system_real, system_imag, sys_index, local):
    states = system_real.shape[0]
    rows = one_hot((local, states), lambda row, col: col == row + local * sys_index)
    real = picked(rows, symmetric_tile(system_real, 1.0))
    imag = picked(rows, symmetric_tile(system_imag, -1.0))

    def place(part):
        def hit(row, col):
            block = col // local
            side = jnp.where(block < 2, sys_index, 1 - sys_index)
            return (block % 2 == part) & (row == col % local + local * side)

        return one_hot((states, 2 * states), hit)

    to_real, to_imag = place(0), place(1)
    upper = product(imag, to_real) + product(real, to_imag)
    lower = product(imag, to_imag) - product(real, to_real)
    return jnp.concatenate([upper, lower], axis=0).astype(jnp.bfloat16)


def section_kernel(
    count,
    dens,
    system_real,
    system_imag,
    left_ham,
    left_coupling,
    right_ham,
    right_coupling,
    left_strength,
    right_strength,
    left_damping,
    right_damping,
    energies,
    other,
    left_out,
    mine,
    level,
    taken,
    given,
    rest,
    left_mat,
    right_mat,
    sys_mat,
    fwd_send,
    fwd_recv,
    ret_send,
    ret_recv,
    sys_send,
    sys_recv,
    level_sem,
    mine_sem,
):
    me = lax.axis_index("rc")
    sys_index = lax.axis_index("sys")
    _, halves, half, local, columns = dens.shape
    levels = 2 * half
    row_blocks = local // ROWS
    parts = count // (2 * row_blocks)
    chunks = half // parts
    odd = lax.rem(me, 2)
    partner = me + 1 - 2 * odd
    shared = (halves - 1) * (1 - odd)

    def task(rank, chunk):
        part = rank // (row_blocks * parts)
        row = lax.rem(rank // parts, row_blocks) * ROWS
        return part, lax.rem(rank, parts) * chunks + chunk, pl.ds(pl.multiple_of(row, ROWS), ROWS)

    def peer(turn):
        side = count // 2
        other_side = lax.rem(turn, 2)
        return lax.rem(me // side + other_side, 2) * side + lax.rem(me + turn // 2, side)

    def part_of(rank, chunk):
        part, at, row = task(rank, chunk)
        return dens.at[part, :, at, row, :]

    def forward(chunk, rank, owner):
        return pltpu.make_async_remote_copy(
            src_ref=part_of(rank, chunk),
            dst_ref=taken.at[chunk, pl.ds(owner * halves, halves)],
            send_sem=fwd_send.at[chunk, rank],
            recv_sem=fwd_recv.at[chunk, owner],
            device_id={"rc": rank},
            device_id_type=pl.DeviceIdType.MESH,
        )

    def forward_own(chunk):
        return pltpu.make_async_copy(
            part_of(me, chunk), taken.at[chunk, pl.ds(me * halves, halves)], fwd_recv.at[chunk, me]
        )

    def landing(rank, chunk):
        part, at, row = task(rank, chunk)
        return left_out.at[1 - part, :, at, row, :]

    def giveback(chunk, rank, worker):
        return pltpu.make_async_remote_copy(
            src_ref=given.at[chunk, pl.ds(rank * halves, halves)],
            dst_ref=landing(worker, chunk),
            send_sem=ret_send.at[chunk, rank],
            recv_sem=ret_recv.at[chunk, worker],
            device_id={"rc": rank},
            device_id_type=pl.DeviceIdType.MESH,
        )

    def giveback_own(chunk):
        return pltpu.make_async_copy(
            given.at[chunk, pl.ds(me * halves, halves)], landing(me, chunk), ret_recv.at[chunk, me]
        )

    def swap(index):
        return pltpu.make_async_remote_copy(
            src_ref=dens.at[:, index],
            dst_ref=other.at[:, index],
            send_sem=sys_send.at[index],
            recv_sem=sys_recv.at[index],
            device_id={"sys": 1 - sys_index},
            device_id_type=pl.DeviceIdType.MESH,
        )

    barrier = pltpu.get_barrier_semaphore()

    @pl.loop(1, count)
    def _(offset):
        pl.semaphore_signal(
            barrier, inc=1, device_id={"rc": peer(offset)}, device_id_type=pl.DeviceIdType.MESH
        )

    pl.semaphore_signal(
        barrier, inc=1, device_id={"sys": 1 - sys_index}, device_id_type=pl.DeviceIdType.MESH
    )
    pl.semaphore_wait(barrier, count)

    level_copy = pltpu.make_async_remote_copy(
        src_ref=dens.at[:, shared],
        dst_ref=level.at[:, odd],
        send_sem=level_sem.at[0],
        recv_sem=level_sem.at[1],
        device_id={"rc": partner},
        device_id_type=pl.DeviceIdType.MESH,
    )
    level_copy.start()
    level_own = pltpu.make_async_copy(dens.at[:, shared], level.at[:, odd], level_sem.at[2])
    level_own.start()
    mine_copy = pltpu.make_async_copy(dens, mine, mine_sem)
    mine_copy.start()

    def send(chunk):
        forward_own(chunk).start()

        @pl.loop(1, count)
        def _(offset):
            forward(chunk, peer(offset), me).start()

        swap(chunk).start()

    @pl.loop(0, AHEAD)
    def _(chunk):
        send(chunk)

    my_part = me // (row_blocks * parts)
    my_row = lax.rem(me // parts, row_blocks) * ROWS
    left_mat[...] = ladder_matrix(
        left_ham[...], left_coupling[...], left_strength[...], sys_index * local + my_row
    )
    for block in range(row_blocks):
        right_mat[block] = ladder_matrix(
            right_ham[...],
            right_coupling[...],
            right_strength[...],
            sys_index * local + block * ROWS,
        )
    sys_mat[...] = system_matrix(system_real[...], system_imag[...], sys_index, local)

    mine_copy.wait()
    level_own.wait()
    level_copy.wait()
    full_levels = halves // 2

    @pl.loop(0, 2)
    def _(part):
        sign = jnp.where(part == 1, 1.0, -1.0)
        for block in range(row_blocks):
            row = pl.ds(block * ROWS, ROWS)

            @pl.loop(0, full_levels)
            def _(number):
                first = odd + 2 * number
                held = mine[part, pl.ds(first, 2), :, row, :].reshape(levels * ROWS, columns)
                term = product(right_mat[block], held) * sign
                rest[1 - part, pl.ds(first, 2), :, row, :] = term.reshape(2, half, ROWS, columns)

            held = level[part, :, :, row, :].reshape(levels * ROWS, columns)
            rows = pl.ds(pl.multiple_of(odd * half * ROWS, half * ROWS), half * ROWS)
            term = product(right_mat[block, rows, :], held) * sign
            rest[1 - part, shared, :, row, :] = term.reshape(half, ROWS, columns)

    def system_rows(index):
        swap(index).wait_recv()

        @pl.loop(0, half)
        def _(at):
            pair = (me * halves + index) * half + at
            damping = 0.5 * (left_damping[pair // levels] + right_damping[lax.rem(pair, levels)])
            real, imag = mine[0, index, at], mine[1, index, at]
            held = jnp.concatenate([real, imag, other[0, index, at], other[1, index, at]], axis=0)
            term = product(sys_mat[...], held)
            real, imag = real.astype(jnp.float32), imag.astype(jnp.float32)
            energy = energies[...]
            new_real = term[:local] + rest[0, index, at] - energy * imag - damping * real
            new_imag = term[local:] + rest[1, index, at] + energy * real - damping * imag
            other[0, index, at] = new_real.astype(jnp.bfloat16)
            other[1, index, at] = new_imag.astype(jnp.bfloat16)

    my_sign = jnp.where(my_part == 1, 1.0, -1.0)

    @pl.loop(0, chunks)
    def _(chunk):
        forward_own(chunk).wait()

        @pl.loop(1, count)
        def _(offset):
            forward(chunk, me, peer(offset)).wait_recv()

        @pl.when(chunk + AHEAD < chunks)
        def _():
            send(chunk + AHEAD)

        for side in range(2):
            held = jnp.concatenate(
                [taken[chunk, 2 * number + side] for number in range(levels)], axis=0
            )
            term = (product(left_mat[...], held) * my_sign).astype(jnp.bfloat16)
            for number in range(levels):
                given[chunk, 2 * number + side] = term[number * ROWS : (number + 1) * ROWS]
        giveback_own(chunk).start()

        @pl.loop(1, count)
        def _(offset):
            giveback(chunk, peer(offset), me).start()

        @pl.when(chunk > 0)
        def _():
            system_rows(chunk - 1)

    @pl.loop(chunks, halves)
    def _(index):
        swap(index).start()

    @pl.loop(chunks - 1, halves)
    def _(index):
        system_rows(index)

    @pl.loop(0, halves)
    def _(index):
        swap(index).wait_send()

    @pl.loop(0, chunks)
    def _(chunk):
        giveback_own(chunk).wait()

        @pl.loop(1, count)
        def _(offset):
            rank = peer(offset)
            forward(chunk, rank, me).wait_send()
            giveback(chunk, rank, me).wait_send()
            giveback(chunk, me, rank).wait_recv()


def add_kernel(rest, left, total, staged, sems):
    _, halves = rest.shape[:2]

    def out(part, index):
        return pltpu.make_async_copy(
            staged.at[part, index], total.at[part, index], sems.at[part, index]
        )

    for part in range(2):

        @pl.loop(0, halves)
        def _(index):
            summed = rest[part, index].astype(jnp.float32) + left[part, index].astype(jnp.float32)
            staged[part, index] = summed.astype(jnp.bfloat16)
            out(part, index).start()

    for part in range(2):

        @pl.loop(0, halves)
        def _(index):
            out(part, index).wait()


def exchanged(
    density,
    system_real,
    system_imag,
    left_ham,
    left_coupling,
    right_ham,
    right_coupling,
    left_strength,
    right_strength,
    left_damping,
    right_damping,
    energies,
):
    count = lax.axis_size("rc")
    levels = left_ham.shape[0]
    half = levels // 2
    _, local, pairs, columns = density.shape
    halves = pairs // half
    size = levels * ROWS
    row_blocks = local // ROWS
    chunks = half * 2 * row_blocks // count
    dens = jnp.transpose(density, (0, 2, 1, 3)).reshape(2, halves, half, local, columns)
    whole = pl.BlockSpec(memory_space=pltpu.VMEM)
    scalars = pl.BlockSpec(memory_space=pltpu.SMEM)
    anywhere = pl.BlockSpec(memory_space=pl.ANY)
    slab = jax.ShapeDtypeStruct(dens.shape, jnp.bfloat16)
    rest, left = pl.pallas_call(
        functools.partial(section_kernel, count),
        out_shape=[pltpu.VMEM(dens.shape, jnp.bfloat16)] * 2,
        in_specs=[anywhere] + [whole] * 8 + [scalars] * 2 + [whole],
        out_specs=[whole, whole],
        scratch_shapes=[
            pltpu.VMEM(dens.shape, jnp.bfloat16),
            pltpu.VMEM((2, 2, half, local, columns), jnp.bfloat16),
            pltpu.VMEM((chunks, count * halves, ROWS, columns), jnp.bfloat16),
            pltpu.VMEM((chunks, count * halves, ROWS, columns), jnp.bfloat16),
            pltpu.VMEM(dens.shape, jnp.float32),
            pltpu.VMEM((size, size), jnp.bfloat16),
            pltpu.VMEM((row_blocks, size, size), jnp.bfloat16),
            pltpu.VMEM((2 * local, 4 * local), jnp.bfloat16),
            pltpu.SemaphoreType.DMA((chunks, count)),
            pltpu.SemaphoreType.DMA((chunks, count)),
            pltpu.SemaphoreType.DMA((chunks, count)),
            pltpu.SemaphoreType.DMA((chunks, count)),
            pltpu.SemaphoreType.DMA((halves,)),
            pltpu.SemaphoreType.DMA((halves,)),
            pltpu.SemaphoreType.DMA((3,)),
            pltpu.SemaphoreType.DMA,
        ],
        compiler_params=pltpu.CompilerParams(
            collective_id=0, has_side_effects=True, vmem_limit_bytes=46 * 2**20
        ),
        cost_estimate=pl.CostEstimate(
            flops=10 * 10**9, bytes_accessed=5 * dens.size * 2, transcendentals=0
        ),
    )(
        dens,
        system_real,
        system_imag,
        left_ham,
        left_coupling,
        right_ham,
        right_coupling,
        left_strength[None, :],
        right_strength[None, :],
        left_damping,
        right_damping,
        energies[None, :],
    )
    total = pl.pallas_call(
        add_kernel,
        out_shape=slab,
        in_specs=[whole, whole],
        out_specs=anywhere,
        scratch_shapes=[
            pltpu.VMEM(dens.shape, jnp.bfloat16),
            pltpu.SemaphoreType.DMA((2, halves)),
        ],
        compiler_params=pltpu.CompilerParams(vmem_limit_bytes=32 * 2**20),
        cost_estimate=pl.CostEstimate(
            flops=dens.size, bytes_accessed=dens.size * 2, transcendentals=0
        ),
    )(rest, left)
    return jnp.transpose(total.reshape(2, pairs, local, columns), (0, 2, 1, 3))


def fits(mesh, shapes):
    count, sides = mesh.shape["rc"], mesh.shape["sys"]
    _, states, pairs, columns = shapes[0]
    levels = shapes[3][0]
    if sides != 2 or levels % 2 or pairs % count or states % (2 * ROWS) or columns % LANES:
        return False
    half, local_pairs = levels // 2, pairs // count
    row_parts = 2 * (states // (2 * ROWS))
    if count % row_parts or half % (count // row_parts) or local_pairs % half:
        return False
    halves, chunks = local_pairs // half, half * row_parts // count
    return halves % 2 == 1 and halves >= chunks >= AHEAD


def solution(mesh):
    placed = (P(None, "sys", "rc", None), P(), P(), P(), P(), P(), P(), P(), P(), P(), P(), P())

    def run(*arrays):
        body = exchanged if fits(mesh, [array.shape for array in arrays]) else shards
        return jax.shard_map(
            body, mesh=mesh, in_specs=placed, out_specs=P(None, "sys", "rc", None), check_vma=False
        )(*arrays)

    return run
```

```python
import functools
import math

import jax
import jax.numpy as jnp
from jax import lax
from jax.experimental import pallas as pl
from jax.experimental.pallas import tpu as pltpu
from jax.sharding import PartitionSpec as P

ROWS = 16
LANES = 128
PIECE = 2
AHEAD = 2


def symmetric(matrix, factor):
    widened = matrix.astype(jnp.float32)
    return ((widened + factor * widened.T) * 0.5).astype(jnp.bfloat16)


def ladder_local(regrouped, left_ops, right_ops, left_gain, right_gain, levels):
    item_count, group_count, all_pairs, column_count = regrouped.shape
    widened = regrouped.reshape(item_count, group_count, levels, levels * column_count)
    left_all = jnp.einsum("xa,ksam->ksxm", left_ops, widened, preferred_element_type=jnp.float32)
    left_term = left_all[:, :, :levels] + left_gain[None, :, None, None] * left_all[:, :, levels:]
    deepened = regrouped.reshape(item_count, group_count, levels, levels, column_count)
    right_all = jnp.einsum(
        "yb,ksabc->ksayc", right_ops, deepened, preferred_element_type=jnp.float32
    )
    right_term = (
        right_all[:, :, :, :levels]
        + right_gain[None, :, None, None, None] * right_all[:, :, :, levels:]
    )
    summed = left_term.reshape(
        item_count, group_count, all_pairs, column_count
    ) + right_term.reshape(item_count, group_count, all_pairs, column_count)
    return summed.astype(jnp.bfloat16)


def shards(
    density,
    system_real,
    system_imag,
    left_ham,
    left_coupling,
    right_ham,
    right_coupling,
    left_strength,
    right_strength,
    left_damping,
    right_damping,
    energies,
):
    herm_real = symmetric(system_real, 1.0)
    herm_imag = symmetric(system_imag, -1.0)
    levels = left_ham.shape[0]
    left_ops = jnp.concatenate([symmetric(left_ham, 1.0), symmetric(left_coupling, 1.0)], axis=0)
    right_ops = jnp.concatenate([symmetric(right_ham, 1.0), symmetric(right_coupling, 1.0)], axis=0)
    state_count = density.shape[1]
    pair_count = density.shape[2]
    column_total = density.shape[3]
    first_state = lax.axis_index("sys") * state_count
    left_gain = lax.dynamic_slice_in_dim(left_strength, first_state, state_count)
    right_gain = lax.dynamic_slice_in_dim(right_strength, first_state, state_count)
    regrouped = lax.all_to_all(density, "sys", split_axis=3, concat_axis=1, tiled=True)
    flattened = regrouped.reshape(2, regrouped.shape[1], -1)
    real_part = jnp.dot(herm_real, flattened[0], preferred_element_type=jnp.float32) - jnp.dot(
        herm_imag, flattened[1], preferred_element_type=jnp.float32
    )
    imag_part = jnp.dot(herm_real, flattened[1], preferred_element_type=jnp.float32) + jnp.dot(
        herm_imag, flattened[0], preferred_element_type=jnp.float32
    )
    product = jnp.stack([real_part, imag_part]).astype(jnp.bfloat16).reshape(regrouped.shape)
    system_rows = lax.all_to_all(product, "sys", split_axis=1, concat_axis=3, tiled=True)
    rc_count = lax.axis_size("rc")
    col_groups = rc_count // math.gcd(state_count, rc_count)
    per_device = state_count * col_groups // rc_count
    group_width = column_total // col_groups
    combined = jnp.moveaxis(
        density.reshape(2, state_count, pair_count, col_groups, group_width), 3, 2
    )
    combined = combined.reshape(2, state_count * col_groups, pair_count, group_width)
    combo_index = lax.axis_index("rc") * per_device + jnp.arange(per_device, dtype=jnp.int32)
    state_pick = (
        (combo_index // col_groups)[:, None] == jnp.arange(state_count, dtype=jnp.int32)[None, :]
    ).astype(jnp.float32)
    combo_left = jnp.sum(state_pick * left_gain[None, :], axis=1)
    combo_right = jnp.sum(state_pick * right_gain[None, :], axis=1)
    summed = ladder_local(
        lax.all_to_all(combined, "rc", split_axis=1, concat_axis=2, tiled=True),
        left_ops,
        right_ops,
        combo_left,
        combo_right,
        levels,
    )
    returned = lax.all_to_all(summed, "rc", split_axis=2, concat_axis=1, tiled=True)
    returned = returned.reshape(2, state_count, col_groups, pair_count, group_width)
    ladder_rows = jnp.moveaxis(returned, 2, 3).reshape(2, state_count, pair_count, column_total)
    pair_index = lax.axis_index("rc") * pair_count + jnp.arange(pair_count, dtype=jnp.int32)
    level_index = jnp.arange(levels, dtype=jnp.int32)
    left_pick = (pair_index[:, None] // levels == level_index[None, :]).astype(jnp.float32)
    right_pick = (pair_index[:, None] % levels == level_index[None, :]).astype(jnp.float32)
    damping = 0.5 * (
        jnp.sum(left_pick * left_damping[None, :], axis=1)
        + jnp.sum(right_pick * right_damping[None, :], axis=1)
    )
    system_term = system_rows.astype(jnp.float32)
    ladder = ladder_rows.astype(jnp.float32)
    real_in = density[0].astype(jnp.float32)
    imag_in = density[1].astype(jnp.float32)
    energy_grid = energies[None, None, :]
    damp_grid = damping[None, :, None]
    new_real = system_term[1] + ladder[1] - energy_grid * imag_in - damp_grid * real_in
    new_imag = -system_term[0] - ladder[0] + energy_grid * real_in - damp_grid * imag_in
    return jnp.stack([new_real, new_imag]).astype(jnp.bfloat16)


def one_hot(shape, hit):
    row = lax.broadcasted_iota(jnp.int32, shape, 0)
    col = lax.broadcasted_iota(jnp.int32, shape, 1)
    return jnp.where(hit(row, col), 1.0, 0.0).astype(jnp.bfloat16)


def product(left, right):
    return jnp.dot(left, right, preferred_element_type=jnp.float32)


def picked(left, right):
    return product(left, right).astype(jnp.bfloat16)


def symmetric_tile(matrix, factor):
    size = matrix.shape[0]
    eye = one_hot((size, size), lambda row, col: row == col)
    turned = lax.dot_general(
        matrix, eye, (((0,), (0,)), ((), ())), preferred_element_type=jnp.float32
    )
    return ((matrix.astype(jnp.float32) + factor * turned) * 0.5).astype(jnp.bfloat16)


def ladder_matrix(ham, coupling, strength, first_state):
    levels = ham.shape[0]
    size = levels * ROWS
    tall = one_hot((size, levels), lambda row, col: row // ROWS == col)
    wide = one_hot((levels, size), lambda row, col: row == col // ROWS)
    ham_all = product(picked(tall, symmetric_tile(ham, 1.0)), wide)
    coupling_all = product(picked(tall, symmetric_tile(coupling, 1.0)), wide)
    states = strength.shape[1]
    row = lax.broadcasted_iota(jnp.int32, (size, states), 0)
    col = lax.broadcasted_iota(jnp.int32, (size, states), 1)
    gain = jnp.sum(
        jnp.where(col == first_state + row % ROWS, strength, 0.0), axis=1, keepdims=True
    )
    row = lax.broadcasted_iota(jnp.int32, (size, size), 0)
    col = lax.broadcasted_iota(jnp.int32, (size, size), 1)
    mixed = ham_all + gain * coupling_all
    return jnp.where(row % ROWS == col % ROWS, mixed, 0.0).astype(jnp.bfloat16)


def system_matrix(system_real, system_imag, sys_index, local):
    states = system_real.shape[0]
    rows = one_hot((local, states), lambda row, col: col == row + local * sys_index)
    real = picked(rows, symmetric_tile(system_real, 1.0))
    imag = picked(rows, symmetric_tile(system_imag, -1.0))

    def place(part):
        def hit(row, col):
            block = col // local
            side = jnp.where(block < 2, sys_index, 1 - sys_index)
            return (block % 2 == part) & (row == col % local + local * side)

        return one_hot((states, 2 * states), hit)

    to_real, to_imag = place(0), place(1)
    upper = product(imag, to_real) + product(real, to_imag)
    lower = product(imag, to_imag) - product(real, to_real)
    return jnp.concatenate([upper, lower], axis=0).astype(jnp.bfloat16)


def section_kernel(
    count,
    dens,
    system_real,
    system_imag,
    left_ham,
    left_coupling,
    right_ham,
    right_coupling,
    left_strength,
    right_strength,
    left_damping,
    right_damping,
    energies,
    other,
    left_out,
    mine,
    level,
    taken,
    given,
    rest,
    left_mat,
    right_mat,
    sys_mat,
    fwd_send,
    fwd_recv,
    ret_send,
    ret_recv,
    sys_send,
    sys_recv,
    level_sem,
    mine_sem,
):
    me = lax.axis_index("rc")
    sys_index = lax.axis_index("sys")
    _, halves, half, local, columns = dens.shape
    levels = 2 * half
    row_blocks = local // ROWS
    parts = count // (2 * row_blocks)
    chunks = half // parts
    odd = lax.rem(me, 2)
    partner = me + 1 - 2 * odd
    shared = (halves - 1) * (1 - odd)

    def task(rank, chunk):
        part = rank // (row_blocks * parts)
        row = lax.rem(rank // parts, row_blocks) * ROWS
        return part, lax.rem(rank, parts) * chunks + chunk, pl.ds(pl.multiple_of(row, ROWS), ROWS)

    def peer(turn):
        side = count // 2
        other_side = lax.rem(turn, 2)
        return lax.rem(me // side + other_side, 2) * side + lax.rem(me + turn // 2, side)

    def part_of(rank, chunk):
        part, at, row = task(rank, chunk)
        return dens.at[part, :, at, row, :]

    def forward(chunk, rank, owner):
        return pltpu.make_async_remote_copy(
            src_ref=part_of(rank, chunk),
            dst_ref=taken.at[chunk, pl.ds(owner * halves, halves)],
            send_sem=fwd_send.at[chunk, rank],
            recv_sem=fwd_recv.at[chunk, owner],
            device_id={"rc": rank},
            device_id_type=pl.DeviceIdType.MESH,
        )

    def forward_own(chunk):
        return pltpu.make_async_copy(
            part_of(me, chunk), taken.at[chunk, pl.ds(me * halves, halves)], fwd_recv.at[chunk, me]
        )

    def landing(rank, chunk):
        part, at, row = task(rank, chunk)
        return left_out.at[1 - part, :, at, row, :]

    def giveback(chunk, rank, worker):
        return pltpu.make_async_remote_copy(
            src_ref=given.at[chunk, pl.ds(rank * halves, halves)],
            dst_ref=landing(worker, chunk),
            send_sem=ret_send.at[chunk, rank],
            recv_sem=ret_recv.at[chunk, worker],
            device_id={"rc": rank},
            device_id_type=pl.DeviceIdType.MESH,
        )

    def giveback_own(chunk):
        return pltpu.make_async_copy(
            given.at[chunk, pl.ds(me * halves, halves)], landing(me, chunk), ret_recv.at[chunk, me]
        )

    def swap(index):
        return pltpu.make_async_remote_copy(
            src_ref=dens.at[:, index],
            dst_ref=other.at[:, index],
            send_sem=sys_send.at[index],
            recv_sem=sys_recv.at[index],
            device_id={"sys": 1 - sys_index},
            device_id_type=pl.DeviceIdType.MESH,
        )

    def swap_piece(index, piece):
        held = (slice(None), index, pl.ds(piece * PIECE, PIECE))
        return pltpu.make_async_remote_copy(
            src_ref=dens.at[held],
            dst_ref=other.at[held],
            send_sem=sys_send.at[index],
            recv_sem=sys_recv.at[index],
            device_id={"sys": 1 - sys_index},
            device_id_type=pl.DeviceIdType.MESH,
        )

    barrier = pltpu.get_barrier_semaphore()

    @pl.loop(1, count)
    def _(offset):
        pl.semaphore_signal(
            barrier, inc=1, device_id={"rc": peer(offset)}, device_id_type=pl.DeviceIdType.MESH
        )

    pl.semaphore_signal(
        barrier, inc=1, device_id={"sys": 1 - sys_index}, device_id_type=pl.DeviceIdType.MESH
    )
    pl.semaphore_wait(barrier, count)

    level_copy = pltpu.make_async_remote_copy(
        src_ref=dens.at[:, shared],
        dst_ref=level.at[:, odd],
        send_sem=level_sem.at[0],
        recv_sem=level_sem.at[1],
        device_id={"rc": partner},
        device_id_type=pl.DeviceIdType.MESH,
    )
    level_copy.start()
    level_own = pltpu.make_async_copy(dens.at[:, shared], level.at[:, odd], level_sem.at[2])
    level_own.start()
    mine_copy = pltpu.make_async_copy(dens, mine, mine_sem)
    mine_copy.start()

    def send(chunk):
        forward_own(chunk).start()

        @pl.loop(1, count)
        def _(offset):
            forward(chunk, peer(offset), me).start()

            @pl.when(offset <= half // PIECE)
            def _():
                swap_piece(chunk, offset - 1).start()

    @pl.loop(0, AHEAD)
    def _(chunk):
        send(chunk)

    my_part = me // (row_blocks * parts)
    my_row = lax.rem(me // parts, row_blocks) * ROWS
    left_mat[...] = ladder_matrix(
        left_ham[...], left_coupling[...], left_strength[...], sys_index * local + my_row
    )
    for block in range(row_blocks):
        right_mat[block] = ladder_matrix(
            right_ham[...],
            right_coupling[...],
            right_strength[...],
            sys_index * local + block * ROWS,
        )
    sys_mat[...] = system_matrix(system_real[...], system_imag[...], sys_index, local)

    mine_copy.wait()
    level_own.wait()
    level_copy.wait()
    full_levels = halves // 2

    @pl.loop(0, 2)
    def _(part):
        sign = jnp.where(part == 1, 1.0, -1.0)
        for block in range(row_blocks):
            row = pl.ds(block * ROWS, ROWS)

            @pl.loop(0, full_levels)
            def _(number):
                first = odd + 2 * number
                held = mine[part, pl.ds(first, 2), :, row, :].reshape(levels * ROWS, columns)
                term = product(right_mat[block], held) * sign
                rest[1 - part, pl.ds(first, 2), :, row, :] = term.reshape(2, half, ROWS, columns)

            held = level[part, :, :, row, :].reshape(levels * ROWS, columns)
            rows = pl.ds(pl.multiple_of(odd * half * ROWS, half * ROWS), half * ROWS)
            term = product(right_mat[block, rows, :], held) * sign
            rest[1 - part, shared, :, row, :] = term.reshape(half, ROWS, columns)

    def system_rows(index):
        swap(index).wait_recv()

        @pl.loop(0, half)
        def _(at):
            pair = (me * halves + index) * half + at
            damping = 0.5 * (left_damping[pair // levels] + right_damping[lax.rem(pair, levels)])
            real, imag = mine[0, index, at], mine[1, index, at]
            held = jnp.concatenate([real, imag, other[0, index, at], other[1, index, at]], axis=0)
            term = product(sys_mat[...], held)
            real, imag = real.astype(jnp.float32), imag.astype(jnp.float32)
            energy = energies[...]
            new_real = term[:local] + rest[0, index, at] - energy * imag - damping * real
            new_imag = term[local:] + rest[1, index, at] + energy * real - damping * imag
            other[0, index, at] = new_real.astype(jnp.bfloat16)
            other[1, index, at] = new_imag.astype(jnp.bfloat16)

    my_sign = jnp.where(my_part == 1, 1.0, -1.0)

    @pl.loop(0, chunks)
    def _(chunk):
        forward_own(chunk).wait()

        @pl.loop(1, count)
        def _(offset):
            forward(chunk, me, peer(offset)).wait_recv()

        @pl.when(chunk + AHEAD < chunks)
        def _():
            send(chunk + AHEAD)

        for side in range(2):
            held = jnp.concatenate(
                [taken[chunk, 2 * number + side] for number in range(levels)], axis=0
            )
            term = (product(left_mat[...], held) * my_sign).astype(jnp.bfloat16)
            for number in range(levels):
                given[chunk, 2 * number + side] = term[number * ROWS : (number + 1) * ROWS]
        giveback_own(chunk).start()

        @pl.loop(1, count)
        def _(offset):
            giveback(chunk, peer(offset), me).start()

        @pl.when(chunk > 0)
        def _():
            system_rows(chunk - 1)

    @pl.loop(chunks, halves)
    def _(index):
        swap(index).start()

    @pl.loop(chunks - 1, halves)
    def _(index):
        system_rows(index)

    @pl.loop(0, halves)
    def _(index):
        swap(index).wait_send()

    @pl.loop(0, chunks)
    def _(chunk):
        giveback_own(chunk).wait()

        @pl.loop(1, count)
        def _(offset):
            rank = peer(offset)
            forward(chunk, rank, me).wait_send()
            giveback(chunk, rank, me).wait_send()
            giveback(chunk, me, rank).wait_recv()


def add_kernel(rest, left, total, staged, sems):
    _, halves = rest.shape[:2]

    def out(part, index):
        return pltpu.make_async_copy(
            staged.at[part, index], total.at[part, index], sems.at[part, index]
        )

    for part in range(2):

        @pl.loop(0, halves)
        def _(index):
            summed = rest[part, index].astype(jnp.float32) + left[part, index].astype(jnp.float32)
            staged[part, index] = summed.astype(jnp.bfloat16)
            out(part, index).start()

    for part in range(2):

        @pl.loop(0, halves)
        def _(index):
            out(part, index).wait()


def exchanged(
    density,
    system_real,
    system_imag,
    left_ham,
    left_coupling,
    right_ham,
    right_coupling,
    left_strength,
    right_strength,
    left_damping,
    right_damping,
    energies,
):
    count = lax.axis_size("rc")
    levels = left_ham.shape[0]
    half = levels // 2
    _, local, pairs, columns = density.shape
    halves = pairs // half
    size = levels * ROWS
    row_blocks = local // ROWS
    chunks = half * 2 * row_blocks // count
    dens = jnp.transpose(density, (0, 2, 1, 3)).reshape(2, halves, half, local, columns)
    whole = pl.BlockSpec(memory_space=pltpu.VMEM)
    scalars = pl.BlockSpec(memory_space=pltpu.SMEM)
    anywhere = pl.BlockSpec(memory_space=pl.ANY)
    slab = jax.ShapeDtypeStruct(dens.shape, jnp.bfloat16)
    rest, left = pl.pallas_call(
        functools.partial(section_kernel, count),
        out_shape=[pltpu.VMEM(dens.shape, jnp.bfloat16)] * 2,
        in_specs=[anywhere] + [whole] * 8 + [scalars] * 2 + [whole],
        out_specs=[whole, whole],
        scratch_shapes=[
            pltpu.VMEM(dens.shape, jnp.bfloat16),
            pltpu.VMEM((2, 2, half, local, columns), jnp.bfloat16),
            pltpu.VMEM((chunks, count * halves, ROWS, columns), jnp.bfloat16),
            pltpu.VMEM((chunks, count * halves, ROWS, columns), jnp.bfloat16),
            pltpu.VMEM(dens.shape, jnp.float32),
            pltpu.VMEM((size, size), jnp.bfloat16),
            pltpu.VMEM((row_blocks, size, size), jnp.bfloat16),
            pltpu.VMEM((2 * local, 4 * local), jnp.bfloat16),
            pltpu.SemaphoreType.DMA((chunks, count)),
            pltpu.SemaphoreType.DMA((chunks, count)),
            pltpu.SemaphoreType.DMA((chunks, count)),
            pltpu.SemaphoreType.DMA((chunks, count)),
            pltpu.SemaphoreType.DMA((halves,)),
            pltpu.SemaphoreType.DMA((halves,)),
            pltpu.SemaphoreType.DMA((3,)),
            pltpu.SemaphoreType.DMA,
        ],
        compiler_params=pltpu.CompilerParams(
            collective_id=0, has_side_effects=True, vmem_limit_bytes=46 * 2**20
        ),
        cost_estimate=pl.CostEstimate(
            flops=10 * 10**9, bytes_accessed=5 * dens.size * 2, transcendentals=0
        ),
    )(
        dens,
        system_real,
        system_imag,
        left_ham,
        left_coupling,
        right_ham,
        right_coupling,
        left_strength[None, :],
        right_strength[None, :],
        left_damping,
        right_damping,
        energies[None, :],
    )
    total = pl.pallas_call(
        add_kernel,
        out_shape=slab,
        in_specs=[whole, whole],
        out_specs=anywhere,
        scratch_shapes=[
            pltpu.VMEM(dens.shape, jnp.bfloat16),
            pltpu.SemaphoreType.DMA((2, halves)),
        ],
        compiler_params=pltpu.CompilerParams(vmem_limit_bytes=32 * 2**20),
        cost_estimate=pl.CostEstimate(
            flops=dens.size, bytes_accessed=dens.size * 2, transcendentals=0
        ),
    )(rest, left)
    return jnp.transpose(total.reshape(2, pairs, local, columns), (0, 2, 1, 3))


def fits(mesh, shapes):
    count, sides = mesh.shape["rc"], mesh.shape["sys"]
    _, states, pairs, columns = shapes[0]
    levels = shapes[3][0]
    if sides != 2 or levels % 2 or pairs % count or states % (2 * ROWS) or columns % LANES:
        return False
    half, local_pairs = levels // 2, pairs // count
    row_parts = 2 * (states // (2 * ROWS))
    if half % PIECE or half // PIECE >= count:
        return False
    if count % row_parts or half % (count // row_parts) or local_pairs % half:
        return False
    halves, chunks = local_pairs // half, half * row_parts // count
    return halves % 2 == 1 and halves >= chunks >= AHEAD


def solution(mesh):
    placed = (P(None, "sys", "rc", None), P(), P(), P(), P(), P(), P(), P(), P(), P(), P(), P())

    def run(*arrays):
        body = exchanged if fits(mesh, [array.shape for array in arrays]) else shards
        return jax.shard_map(
            body, mesh=mesh, in_specs=placed, out_specs=P(None, "sys", "rc", None), check_vma=False
        )(*arrays)

    return run
```

```python
import functools
import math

import jax
import jax.numpy as jnp
from jax import lax
from jax.experimental import pallas as pl
from jax.experimental.pallas import tpu as pltpu
from jax.sharding import PartitionSpec as P

ROWS = 16
LANES = 128
PIECE = 2
AHEAD = 2


def symmetric(matrix, factor):
    widened = matrix.astype(jnp.float32)
    return ((widened + factor * widened.T) * 0.5).astype(jnp.bfloat16)


def ladder_local(regrouped, left_ops, right_ops, left_gain, right_gain, levels):
    item_count, group_count, all_pairs, column_count = regrouped.shape
    widened = regrouped.reshape(item_count, group_count, levels, levels * column_count)
    left_all = jnp.einsum("xa,ksam->ksxm", left_ops, widened, preferred_element_type=jnp.float32)
    left_term = left_all[:, :, :levels] + left_gain[None, :, None, None] * left_all[:, :, levels:]
    deepened = regrouped.reshape(item_count, group_count, levels, levels, column_count)
    right_all = jnp.einsum(
        "yb,ksabc->ksayc", right_ops, deepened, preferred_element_type=jnp.float32
    )
    right_term = (
        right_all[:, :, :, :levels]
        + right_gain[None, :, None, None, None] * right_all[:, :, :, levels:]
    )
    summed = left_term.reshape(
        item_count, group_count, all_pairs, column_count
    ) + right_term.reshape(item_count, group_count, all_pairs, column_count)
    return summed.astype(jnp.bfloat16)


def shards(
    density,
    system_real,
    system_imag,
    left_ham,
    left_coupling,
    right_ham,
    right_coupling,
    left_strength,
    right_strength,
    left_damping,
    right_damping,
    energies,
):
    herm_real = symmetric(system_real, 1.0)
    herm_imag = symmetric(system_imag, -1.0)
    levels = left_ham.shape[0]
    left_ops = jnp.concatenate([symmetric(left_ham, 1.0), symmetric(left_coupling, 1.0)], axis=0)
    right_ops = jnp.concatenate([symmetric(right_ham, 1.0), symmetric(right_coupling, 1.0)], axis=0)
    state_count = density.shape[1]
    pair_count = density.shape[2]
    column_total = density.shape[3]
    first_state = lax.axis_index("sys") * state_count
    left_gain = lax.dynamic_slice_in_dim(left_strength, first_state, state_count)
    right_gain = lax.dynamic_slice_in_dim(right_strength, first_state, state_count)
    regrouped = lax.all_to_all(density, "sys", split_axis=3, concat_axis=1, tiled=True)
    flattened = regrouped.reshape(2, regrouped.shape[1], -1)
    real_part = jnp.dot(herm_real, flattened[0], preferred_element_type=jnp.float32) - jnp.dot(
        herm_imag, flattened[1], preferred_element_type=jnp.float32
    )
    imag_part = jnp.dot(herm_real, flattened[1], preferred_element_type=jnp.float32) + jnp.dot(
        herm_imag, flattened[0], preferred_element_type=jnp.float32
    )
    product = jnp.stack([real_part, imag_part]).astype(jnp.bfloat16).reshape(regrouped.shape)
    system_rows = lax.all_to_all(product, "sys", split_axis=1, concat_axis=3, tiled=True)
    rc_count = lax.axis_size("rc")
    col_groups = rc_count // math.gcd(state_count, rc_count)
    per_device = state_count * col_groups // rc_count
    group_width = column_total // col_groups
    combined = jnp.moveaxis(
        density.reshape(2, state_count, pair_count, col_groups, group_width), 3, 2
    )
    combined = combined.reshape(2, state_count * col_groups, pair_count, group_width)
    combo_index = lax.axis_index("rc") * per_device + jnp.arange(per_device, dtype=jnp.int32)
    state_pick = (
        (combo_index // col_groups)[:, None] == jnp.arange(state_count, dtype=jnp.int32)[None, :]
    ).astype(jnp.float32)
    combo_left = jnp.sum(state_pick * left_gain[None, :], axis=1)
    combo_right = jnp.sum(state_pick * right_gain[None, :], axis=1)
    summed = ladder_local(
        lax.all_to_all(combined, "rc", split_axis=1, concat_axis=2, tiled=True),
        left_ops,
        right_ops,
        combo_left,
        combo_right,
        levels,
    )
    returned = lax.all_to_all(summed, "rc", split_axis=2, concat_axis=1, tiled=True)
    returned = returned.reshape(2, state_count, col_groups, pair_count, group_width)
    ladder_rows = jnp.moveaxis(returned, 2, 3).reshape(2, state_count, pair_count, column_total)
    pair_index = lax.axis_index("rc") * pair_count + jnp.arange(pair_count, dtype=jnp.int32)
    level_index = jnp.arange(levels, dtype=jnp.int32)
    left_pick = (pair_index[:, None] // levels == level_index[None, :]).astype(jnp.float32)
    right_pick = (pair_index[:, None] % levels == level_index[None, :]).astype(jnp.float32)
    damping = 0.5 * (
        jnp.sum(left_pick * left_damping[None, :], axis=1)
        + jnp.sum(right_pick * right_damping[None, :], axis=1)
    )
    system_term = system_rows.astype(jnp.float32)
    ladder = ladder_rows.astype(jnp.float32)
    real_in = density[0].astype(jnp.float32)
    imag_in = density[1].astype(jnp.float32)
    energy_grid = energies[None, None, :]
    damp_grid = damping[None, :, None]
    new_real = system_term[1] + ladder[1] - energy_grid * imag_in - damp_grid * real_in
    new_imag = -system_term[0] - ladder[0] + energy_grid * real_in - damp_grid * imag_in
    return jnp.stack([new_real, new_imag]).astype(jnp.bfloat16)


def one_hot(shape, hit):
    row = lax.broadcasted_iota(jnp.int32, shape, 0)
    col = lax.broadcasted_iota(jnp.int32, shape, 1)
    return jnp.where(hit(row, col), 1.0, 0.0).astype(jnp.bfloat16)


def product(left, right):
    return jnp.dot(left, right, preferred_element_type=jnp.float32)


def picked(left, right):
    return product(left, right).astype(jnp.bfloat16)


def symmetric_tile(matrix, factor):
    size = matrix.shape[0]
    eye = one_hot((size, size), lambda row, col: row == col)
    turned = lax.dot_general(
        matrix, eye, (((0,), (0,)), ((), ())), preferred_element_type=jnp.float32
    )
    return ((matrix.astype(jnp.float32) + factor * turned) * 0.5).astype(jnp.bfloat16)


def ladder_matrix(ham, coupling, strength, first_state):
    levels = ham.shape[0]
    size = levels * ROWS
    tall = one_hot((size, levels), lambda row, col: row // ROWS == col)
    wide = one_hot((levels, size), lambda row, col: row == col // ROWS)
    ham_all = product(picked(tall, symmetric_tile(ham, 1.0)), wide)
    coupling_all = product(picked(tall, symmetric_tile(coupling, 1.0)), wide)
    states = strength.shape[1]
    row = lax.broadcasted_iota(jnp.int32, (size, states), 0)
    col = lax.broadcasted_iota(jnp.int32, (size, states), 1)
    gain = jnp.sum(
        jnp.where(col == first_state + row % ROWS, strength, 0.0), axis=1, keepdims=True
    )
    row = lax.broadcasted_iota(jnp.int32, (size, size), 0)
    col = lax.broadcasted_iota(jnp.int32, (size, size), 1)
    mixed = ham_all + gain * coupling_all
    return jnp.where(row % ROWS == col % ROWS, mixed, 0.0).astype(jnp.bfloat16)


def system_matrix(system_real, system_imag, sys_index, local):
    states = system_real.shape[0]
    rows = one_hot((local, states), lambda row, col: col == row + local * sys_index)
    real = picked(rows, symmetric_tile(system_real, 1.0))
    imag = picked(rows, symmetric_tile(system_imag, -1.0))

    def place(part):
        def hit(row, col):
            block = col // local
            side = jnp.where(block < 2, sys_index, 1 - sys_index)
            return (block % 2 == part) & (row == col % local + local * side)

        return one_hot((states, 2 * states), hit)

    to_real, to_imag = place(0), place(1)
    upper = product(imag, to_real) + product(real, to_imag)
    lower = product(imag, to_imag) - product(real, to_real)
    return jnp.concatenate([upper, lower], axis=0).astype(jnp.bfloat16)


def section_kernel(
    count,
    dens,
    system_real,
    system_imag,
    left_ham,
    left_coupling,
    right_ham,
    right_coupling,
    left_strength,
    right_strength,
    left_damping,
    right_damping,
    energies,
    rest,
    left_out,
    mine,
    other,
    level,
    taken,
    given,
    left_mat,
    right_mat,
    sys_mat,
    fwd_send,
    fwd_recv,
    ret_send,
    ret_recv,
    sys_send,
    sys_recv,
    level_sem,
    mine_sem,
):
    me = lax.axis_index("rc")
    sys_index = lax.axis_index("sys")
    _, halves, half, local, columns = dens.shape
    levels = 2 * half
    row_blocks = local // ROWS
    parts = count // (2 * row_blocks)
    chunks = half // parts
    odd = lax.rem(me, 2)
    partner = me + 1 - 2 * odd
    shared = (halves - 1) * (1 - odd)

    def task(rank, chunk):
        part = rank // (row_blocks * parts)
        row = lax.rem(rank // parts, row_blocks) * ROWS
        return part, lax.rem(rank, parts) * chunks + chunk, pl.ds(pl.multiple_of(row, ROWS), ROWS)

    def peer(turn):
        side = count // 2
        other_side = lax.rem(turn, 2)
        return lax.rem(me // side + other_side, 2) * side + lax.rem(me + turn // 2, side)

    def part_of(rank, chunk):
        part, at, row = task(rank, chunk)
        return dens.at[part, :, at, row, :]

    def forward(chunk, rank, owner):
        return pltpu.make_async_remote_copy(
            src_ref=part_of(rank, chunk),
            dst_ref=taken.at[chunk, pl.ds(owner * halves, halves)],
            send_sem=fwd_send.at[chunk, rank],
            recv_sem=fwd_recv.at[chunk, owner],
            device_id={"rc": rank},
            device_id_type=pl.DeviceIdType.MESH,
        )

    def forward_own(chunk):
        return pltpu.make_async_copy(
            part_of(me, chunk), taken.at[chunk, pl.ds(me * halves, halves)], fwd_recv.at[chunk, me]
        )

    def landing(rank, chunk):
        part, at, row = task(rank, chunk)
        return left_out.at[1 - part, :, at, row, :]

    def giveback(chunk, rank, worker):
        return pltpu.make_async_remote_copy(
            src_ref=given.at[chunk, pl.ds(rank * halves, halves)],
            dst_ref=landing(worker, chunk),
            send_sem=ret_send.at[chunk, rank],
            recv_sem=ret_recv.at[chunk, worker],
            device_id={"rc": rank},
            device_id_type=pl.DeviceIdType.MESH,
        )

    def giveback_own(chunk):
        return pltpu.make_async_copy(
            given.at[chunk, pl.ds(me * halves, halves)], landing(me, chunk), ret_recv.at[chunk, me]
        )

    def swap(index):
        return pltpu.make_async_remote_copy(
            src_ref=dens.at[:, index],
            dst_ref=other.at[:, index],
            send_sem=sys_send.at[index],
            recv_sem=sys_recv.at[index],
            device_id={"sys": 1 - sys_index},
            device_id_type=pl.DeviceIdType.MESH,
        )

    def swap_piece(index, piece):
        held = (slice(None), index, pl.ds(piece * PIECE, PIECE))
        return pltpu.make_async_remote_copy(
            src_ref=dens.at[held],
            dst_ref=other.at[held],
            send_sem=sys_send.at[index],
            recv_sem=sys_recv.at[index],
            device_id={"sys": 1 - sys_index},
            device_id_type=pl.DeviceIdType.MESH,
        )

    barrier = pltpu.get_barrier_semaphore()

    @pl.loop(1, count)
    def _(offset):
        pl.semaphore_signal(
            barrier, inc=1, device_id={"rc": peer(offset)}, device_id_type=pl.DeviceIdType.MESH
        )

    pl.semaphore_signal(
        barrier, inc=1, device_id={"sys": 1 - sys_index}, device_id_type=pl.DeviceIdType.MESH
    )
    pl.semaphore_wait(barrier, count)

    def send(chunk):
        forward_own(chunk).start()

        @pl.loop(1, count)
        def _(offset):
            forward(chunk, peer(offset), me).start()

            @pl.when(offset <= half // PIECE)
            def _():
                swap_piece(chunk, offset - 1).start()

    @pl.loop(0, AHEAD)
    def _(chunk):
        send(chunk)

    level_copy = pltpu.make_async_remote_copy(
        src_ref=dens.at[:, shared],
        dst_ref=level.at[:, odd],
        send_sem=level_sem.at[0],
        recv_sem=level_sem.at[1],
        device_id={"rc": partner},
        device_id_type=pl.DeviceIdType.MESH,
    )
    level_copy.start()
    level_own = pltpu.make_async_copy(dens.at[:, shared], level.at[:, odd], level_sem.at[2])
    level_own.start()
    mine_copy = pltpu.make_async_copy(dens, mine, mine_sem)
    mine_copy.start()

    my_part = me // (row_blocks * parts)
    my_row = lax.rem(me // parts, row_blocks) * ROWS
    left_mat[...] = ladder_matrix(
        left_ham[...], left_coupling[...], left_strength[...], sys_index * local + my_row
    )
    for block in range(row_blocks):
        right_mat[block] = ladder_matrix(
            right_ham[...],
            right_coupling[...],
            right_strength[...],
            sys_index * local + block * ROWS,
        )
    sys_mat[...] = system_matrix(system_real[...], system_imag[...], sys_index, local)

    mine_copy.wait()
    level_own.wait()
    level_copy.wait()
    full_levels = halves // 2

    @pl.loop(0, 2)
    def _(part):
        sign = jnp.where(part == 1, 1.0, -1.0)
        for block in range(row_blocks):
            row = pl.ds(block * ROWS, ROWS)

            @pl.loop(0, full_levels)
            def _(number):
                first = odd + 2 * number
                held = mine[part, pl.ds(first, 2), :, row, :].reshape(levels * ROWS, columns)
                term = product(right_mat[block], held) * sign
                rest[1 - part, pl.ds(first, 2), :, row, :] = term.reshape(2, half, ROWS, columns)

            held = level[part, :, :, row, :].reshape(levels * ROWS, columns)
            rows = pl.ds(pl.multiple_of(odd * half * ROWS, half * ROWS), half * ROWS)
            term = product(right_mat[block, rows, :], held) * sign
            rest[1 - part, shared, :, row, :] = term.reshape(half, ROWS, columns)

    def system_rows(index):
        swap(index).wait_recv()

        @pl.loop(0, half)
        def _(at):
            pair = (me * halves + index) * half + at
            damping = 0.5 * (left_damping[pair // levels] + right_damping[lax.rem(pair, levels)])
            real, imag = mine[0, index, at], mine[1, index, at]
            held = jnp.concatenate([real, imag, other[0, index, at], other[1, index, at]], axis=0)
            term = product(sys_mat[...], held)
            real, imag = real.astype(jnp.float32), imag.astype(jnp.float32)
            energy = energies[...]
            new_real = term[:local] + rest[0, index, at] - energy * imag - damping * real
            new_imag = term[local:] + rest[1, index, at] + energy * real - damping * imag
            rest[0, index, at] = new_real
            rest[1, index, at] = new_imag

    my_sign = jnp.where(my_part == 1, 1.0, -1.0)

    @pl.loop(0, chunks)
    def _(chunk):
        forward_own(chunk).wait()

        @pl.loop(1, count)
        def _(offset):
            forward(chunk, me, peer(offset)).wait_recv()

        @pl.when(chunk + AHEAD < chunks)
        def _():
            send(chunk + AHEAD)

        for side in range(2):
            held = jnp.concatenate(
                [taken[chunk, 2 * number + side] for number in range(levels)], axis=0
            )
            term = (product(left_mat[...], held) * my_sign).astype(jnp.bfloat16)
            for number in range(levels):
                given[chunk, 2 * number + side] = term[number * ROWS : (number + 1) * ROWS]
        giveback_own(chunk).start()

        @pl.loop(1, count)
        def _(offset):
            giveback(chunk, peer(offset), me).start()

        @pl.when(chunk > 0)
        def _():
            system_rows(chunk - 1)

    @pl.loop(chunks, halves)
    def _(index):
        swap(index).start()

    @pl.loop(chunks - 1, halves)
    def _(index):
        system_rows(index)

    @pl.loop(0, halves)
    def _(index):
        swap(index).wait_send()

    @pl.loop(0, chunks)
    def _(chunk):
        giveback_own(chunk).wait()

        @pl.loop(1, count)
        def _(offset):
            rank = peer(offset)
            forward(chunk, rank, me).wait_send()
            giveback(chunk, rank, me).wait_send()
            giveback(chunk, me, rank).wait_recv()


def add_kernel(rest, left, total, staged, sems):
    _, halves = rest.shape[:2]

    def out(part, index):
        return pltpu.make_async_copy(
            staged.at[part, index], total.at[part, index], sems.at[part, index]
        )

    for part in range(2):

        @pl.loop(0, halves)
        def _(index):
            summed = rest[part, index] + left[part, index].astype(jnp.float32)
            staged[part, index] = summed.astype(jnp.bfloat16)
            out(part, index).start()

    for part in range(2):

        @pl.loop(0, halves)
        def _(index):
            out(part, index).wait()


def exchanged(
    density,
    system_real,
    system_imag,
    left_ham,
    left_coupling,
    right_ham,
    right_coupling,
    left_strength,
    right_strength,
    left_damping,
    right_damping,
    energies,
):
    count = lax.axis_size("rc")
    levels = left_ham.shape[0]
    half = levels // 2
    _, local, pairs, columns = density.shape
    halves = pairs // half
    size = levels * ROWS
    row_blocks = local // ROWS
    chunks = half * 2 * row_blocks // count
    dens = jnp.transpose(density, (0, 2, 1, 3)).reshape(2, halves, half, local, columns)
    whole = pl.BlockSpec(memory_space=pltpu.VMEM)
    scalars = pl.BlockSpec(memory_space=pltpu.SMEM)
    anywhere = pl.BlockSpec(memory_space=pl.ANY)
    slab = jax.ShapeDtypeStruct(dens.shape, jnp.bfloat16)
    rest, left = pl.pallas_call(
        functools.partial(section_kernel, count),
        out_shape=[
            pltpu.VMEM(dens.shape, jnp.float32),
            pltpu.VMEM(dens.shape, jnp.bfloat16),
        ],
        in_specs=[anywhere] + [whole] * 8 + [scalars] * 2 + [whole],
        out_specs=[whole, whole],
        scratch_shapes=[
            pltpu.VMEM(dens.shape, jnp.bfloat16),
            pltpu.VMEM(dens.shape, jnp.bfloat16),
            pltpu.VMEM((2, 2, half, local, columns), jnp.bfloat16),
            pltpu.VMEM((chunks, count * halves, ROWS, columns), jnp.bfloat16),
            pltpu.VMEM((chunks, count * halves, ROWS, columns), jnp.bfloat16),
            pltpu.VMEM((size, size), jnp.bfloat16),
            pltpu.VMEM((row_blocks, size, size), jnp.bfloat16),
            pltpu.VMEM((2 * local, 4 * local), jnp.bfloat16),
            pltpu.SemaphoreType.DMA((chunks, count)),
            pltpu.SemaphoreType.DMA((chunks, count)),
            pltpu.SemaphoreType.DMA((chunks, count)),
            pltpu.SemaphoreType.DMA((chunks, count)),
            pltpu.SemaphoreType.DMA((halves,)),
            pltpu.SemaphoreType.DMA((halves,)),
            pltpu.SemaphoreType.DMA((3,)),
            pltpu.SemaphoreType.DMA,
        ],
        compiler_params=pltpu.CompilerParams(
            collective_id=0, has_side_effects=True, vmem_limit_bytes=41 * 2**20
        ),
        cost_estimate=pl.CostEstimate(
            flops=10 * 10**9, bytes_accessed=5 * dens.size * 2, transcendentals=0
        ),
    )(
        dens,
        system_real,
        system_imag,
        left_ham,
        left_coupling,
        right_ham,
        right_coupling,
        left_strength[None, :],
        right_strength[None, :],
        left_damping,
        right_damping,
        energies[None, :],
    )
    total = pl.pallas_call(
        add_kernel,
        out_shape=slab,
        in_specs=[whole, whole],
        out_specs=anywhere,
        scratch_shapes=[
            pltpu.VMEM(dens.shape, jnp.bfloat16),
            pltpu.SemaphoreType.DMA((2, halves)),
        ],
        compiler_params=pltpu.CompilerParams(vmem_limit_bytes=32 * 2**20),
        cost_estimate=pl.CostEstimate(
            flops=dens.size, bytes_accessed=dens.size * 2, transcendentals=0
        ),
    )(rest, left)
    return jnp.transpose(total.reshape(2, pairs, local, columns), (0, 2, 1, 3))


def fits(mesh, shapes):
    count, sides = mesh.shape["rc"], mesh.shape["sys"]
    _, states, pairs, columns = shapes[0]
    levels = shapes[3][0]
    if sides != 2 or levels % 2 or pairs % count or states % (2 * ROWS) or columns % LANES:
        return False
    half, local_pairs = levels // 2, pairs // count
    row_parts = 2 * (states // (2 * ROWS))
    if half % PIECE or half // PIECE >= count:
        return False
    if count % row_parts or half % (count // row_parts) or local_pairs % half:
        return False
    halves, chunks = local_pairs // half, half * row_parts // count
    return halves % 2 == 1 and halves >= chunks >= AHEAD


def solution(mesh):
    placed = (P(None, "sys", "rc", None), P(), P(), P(), P(), P(), P(), P(), P(), P(), P(), P())

    def run(*arrays):
        body = exchanged if fits(mesh, [array.shape for array in arrays]) else shards
        return jax.shard_map(
            body, mesh=mesh, in_specs=placed, out_specs=P(None, "sys", "rc", None), check_vma=False
        )(*arrays)

    return run
```

```python
import functools
import math

import jax
import jax.numpy as jnp
from jax import lax
from jax.experimental import pallas as pl
from jax.experimental.pallas import tpu as pltpu
from jax.sharding import PartitionSpec as P

ROWS = 16
LANES = 128
PIECE = 2
AHEAD = 2


def symmetric(matrix, factor):
    widened = matrix.astype(jnp.float32)
    return ((widened + factor * widened.T) * 0.5).astype(jnp.bfloat16)


def ladder_local(regrouped, left_ops, right_ops, left_gain, right_gain, levels):
    item_count, group_count, all_pairs, column_count = regrouped.shape
    widened = regrouped.reshape(item_count, group_count, levels, levels * column_count)
    left_all = jnp.einsum("xa,ksam->ksxm", left_ops, widened, preferred_element_type=jnp.float32)
    left_term = left_all[:, :, :levels] + left_gain[None, :, None, None] * left_all[:, :, levels:]
    deepened = regrouped.reshape(item_count, group_count, levels, levels, column_count)
    right_all = jnp.einsum(
        "yb,ksabc->ksayc", right_ops, deepened, preferred_element_type=jnp.float32
    )
    right_term = (
        right_all[:, :, :, :levels]
        + right_gain[None, :, None, None, None] * right_all[:, :, :, levels:]
    )
    summed = left_term.reshape(
        item_count, group_count, all_pairs, column_count
    ) + right_term.reshape(item_count, group_count, all_pairs, column_count)
    return summed.astype(jnp.bfloat16)


def shards(
    density,
    system_real,
    system_imag,
    left_ham,
    left_coupling,
    right_ham,
    right_coupling,
    left_strength,
    right_strength,
    left_damping,
    right_damping,
    energies,
):
    herm_real = symmetric(system_real, 1.0)
    herm_imag = symmetric(system_imag, -1.0)
    levels = left_ham.shape[0]
    left_ops = jnp.concatenate([symmetric(left_ham, 1.0), symmetric(left_coupling, 1.0)], axis=0)
    right_ops = jnp.concatenate([symmetric(right_ham, 1.0), symmetric(right_coupling, 1.0)], axis=0)
    state_count = density.shape[1]
    pair_count = density.shape[2]
    column_total = density.shape[3]
    first_state = lax.axis_index("sys") * state_count
    left_gain = lax.dynamic_slice_in_dim(left_strength, first_state, state_count)
    right_gain = lax.dynamic_slice_in_dim(right_strength, first_state, state_count)
    regrouped = lax.all_to_all(density, "sys", split_axis=3, concat_axis=1, tiled=True)
    flattened = regrouped.reshape(2, regrouped.shape[1], -1)
    real_part = jnp.dot(herm_real, flattened[0], preferred_element_type=jnp.float32) - jnp.dot(
        herm_imag, flattened[1], preferred_element_type=jnp.float32
    )
    imag_part = jnp.dot(herm_real, flattened[1], preferred_element_type=jnp.float32) + jnp.dot(
        herm_imag, flattened[0], preferred_element_type=jnp.float32
    )
    product = jnp.stack([real_part, imag_part]).astype(jnp.bfloat16).reshape(regrouped.shape)
    system_rows = lax.all_to_all(product, "sys", split_axis=1, concat_axis=3, tiled=True)
    rc_count = lax.axis_size("rc")
    col_groups = rc_count // math.gcd(state_count, rc_count)
    per_device = state_count * col_groups // rc_count
    group_width = column_total // col_groups
    combined = jnp.moveaxis(
        density.reshape(2, state_count, pair_count, col_groups, group_width), 3, 2
    )
    combined = combined.reshape(2, state_count * col_groups, pair_count, group_width)
    combo_index = lax.axis_index("rc") * per_device + jnp.arange(per_device, dtype=jnp.int32)
    state_pick = (
        (combo_index // col_groups)[:, None] == jnp.arange(state_count, dtype=jnp.int32)[None, :]
    ).astype(jnp.float32)
    combo_left = jnp.sum(state_pick * left_gain[None, :], axis=1)
    combo_right = jnp.sum(state_pick * right_gain[None, :], axis=1)
    summed = ladder_local(
        lax.all_to_all(combined, "rc", split_axis=1, concat_axis=2, tiled=True),
        left_ops,
        right_ops,
        combo_left,
        combo_right,
        levels,
    )
    returned = lax.all_to_all(summed, "rc", split_axis=2, concat_axis=1, tiled=True)
    returned = returned.reshape(2, state_count, col_groups, pair_count, group_width)
    ladder_rows = jnp.moveaxis(returned, 2, 3).reshape(2, state_count, pair_count, column_total)
    pair_index = lax.axis_index("rc") * pair_count + jnp.arange(pair_count, dtype=jnp.int32)
    level_index = jnp.arange(levels, dtype=jnp.int32)
    left_pick = (pair_index[:, None] // levels == level_index[None, :]).astype(jnp.float32)
    right_pick = (pair_index[:, None] % levels == level_index[None, :]).astype(jnp.float32)
    damping = 0.5 * (
        jnp.sum(left_pick * left_damping[None, :], axis=1)
        + jnp.sum(right_pick * right_damping[None, :], axis=1)
    )
    system_term = system_rows.astype(jnp.float32)
    ladder = ladder_rows.astype(jnp.float32)
    real_in = density[0].astype(jnp.float32)
    imag_in = density[1].astype(jnp.float32)
    energy_grid = energies[None, None, :]
    damp_grid = damping[None, :, None]
    new_real = system_term[1] + ladder[1] - energy_grid * imag_in - damp_grid * real_in
    new_imag = -system_term[0] - ladder[0] + energy_grid * real_in - damp_grid * imag_in
    return jnp.stack([new_real, new_imag]).astype(jnp.bfloat16)


def one_hot(shape, hit):
    row = lax.broadcasted_iota(jnp.int32, shape, 0)
    col = lax.broadcasted_iota(jnp.int32, shape, 1)
    return jnp.where(hit(row, col), 1.0, 0.0).astype(jnp.bfloat16)


def product(left, right):
    return jnp.dot(left, right, preferred_element_type=jnp.float32)


def picked(left, right):
    return product(left, right).astype(jnp.bfloat16)


def symmetric_tile(matrix, factor):
    size = matrix.shape[0]
    eye = one_hot((size, size), lambda row, col: row == col)
    turned = lax.dot_general(
        matrix, eye, (((0,), (0,)), ((), ())), preferred_element_type=jnp.float32
    )
    return ((matrix.astype(jnp.float32) + factor * turned) * 0.5).astype(jnp.bfloat16)


def ladder_matrix(ham, coupling, strength, first_state):
    levels = ham.shape[0]
    size = levels * ROWS
    tall = one_hot((size, levels), lambda row, col: row // ROWS == col)
    wide = one_hot((levels, size), lambda row, col: row == col // ROWS)
    ham_all = product(picked(tall, symmetric_tile(ham, 1.0)), wide)
    coupling_all = product(picked(tall, symmetric_tile(coupling, 1.0)), wide)
    states = strength.shape[1]
    row = lax.broadcasted_iota(jnp.int32, (size, states), 0)
    col = lax.broadcasted_iota(jnp.int32, (size, states), 1)
    gain = jnp.sum(
        jnp.where(col == first_state + row % ROWS, strength, 0.0), axis=1, keepdims=True
    )
    row = lax.broadcasted_iota(jnp.int32, (size, size), 0)
    col = lax.broadcasted_iota(jnp.int32, (size, size), 1)
    mixed = ham_all + gain * coupling_all
    return jnp.where(row % ROWS == col % ROWS, mixed, 0.0).astype(jnp.bfloat16)


def system_matrix(system_real, system_imag, sys_index, local):
    states = system_real.shape[0]
    rows = one_hot((local, states), lambda row, col: col == row + local * sys_index)
    real = picked(rows, symmetric_tile(system_real, 1.0))
    imag = picked(rows, symmetric_tile(system_imag, -1.0))

    def place(part):
        def hit(row, col):
            block = col // local
            side = jnp.where(block < 2, sys_index, 1 - sys_index)
            return (block % 2 == part) & (row == col % local + local * side)

        return one_hot((states, 2 * states), hit)

    to_real, to_imag = place(0), place(1)
    upper = product(imag, to_real) + product(real, to_imag)
    lower = product(imag, to_imag) - product(real, to_real)
    return jnp.concatenate([upper, lower], axis=0).astype(jnp.bfloat16)


def section_kernel(
    count,
    dens,
    system_real,
    system_imag,
    left_ham,
    left_coupling,
    right_ham,
    right_coupling,
    left_strength,
    right_strength,
    left_damping,
    right_damping,
    energies,
    rest,
    left_out,
    mine,
    other,
    level,
    taken,
    given,
    left_mat,
    right_mat,
    sys_mat,
    fwd_send,
    fwd_recv,
    ret_send,
    ret_recv,
    sys_send,
    sys_recv,
    level_sem,
    mine_sem,
):
    me = lax.axis_index("rc")
    sys_index = lax.axis_index("sys")
    _, halves, half, local, columns = dens.shape
    levels = 2 * half
    row_blocks = local // ROWS
    parts = count // (2 * row_blocks)
    chunks = half // parts
    odd = lax.rem(me, 2)
    partner = me + 1 - 2 * odd
    shared = (halves - 1) * (1 - odd)

    def task(rank, chunk):
        part = rank // (row_blocks * parts)
        row = lax.rem(rank // parts, row_blocks) * ROWS
        return part, lax.rem(rank, parts) * chunks + chunk, pl.ds(pl.multiple_of(row, ROWS), ROWS)

    def peer(turn):
        side = count // 2
        other_side = lax.rem(turn, 2)
        return lax.rem(me // side + other_side, 2) * side + lax.rem(me + turn // 2, side)

    def part_of(rank, chunk):
        part, at, row = task(rank, chunk)
        return dens.at[part, :, at, row, :]

    def forward(chunk, rank, owner):
        return pltpu.make_async_remote_copy(
            src_ref=part_of(rank, chunk),
            dst_ref=taken.at[chunk, pl.ds(owner * halves, halves)],
            send_sem=fwd_send.at[chunk, rank],
            recv_sem=fwd_recv.at[chunk, owner],
            device_id={"rc": rank},
            device_id_type=pl.DeviceIdType.MESH,
        )

    def forward_own(chunk):
        return pltpu.make_async_copy(
            part_of(me, chunk), taken.at[chunk, pl.ds(me * halves, halves)], fwd_recv.at[chunk, me]
        )

    def landing(rank, chunk):
        part, at, row = task(rank, chunk)
        return left_out.at[1 - part, :, at, row, :]

    def giveback(chunk, rank, worker):
        return pltpu.make_async_remote_copy(
            src_ref=given.at[chunk, pl.ds(rank * halves, halves)],
            dst_ref=landing(worker, chunk),
            send_sem=ret_send.at[chunk, rank],
            recv_sem=ret_recv.at[chunk, worker],
            device_id={"rc": rank},
            device_id_type=pl.DeviceIdType.MESH,
        )

    def giveback_own(chunk):
        return pltpu.make_async_copy(
            given.at[chunk, pl.ds(me * halves, halves)], landing(me, chunk), ret_recv.at[chunk, me]
        )

    def swap(index):
        return pltpu.make_async_remote_copy(
            src_ref=dens.at[:, index],
            dst_ref=other.at[:, index],
            send_sem=sys_send.at[index],
            recv_sem=sys_recv.at[index],
            device_id={"sys": 1 - sys_index},
            device_id_type=pl.DeviceIdType.MESH,
        )

    def swap_piece(index, piece):
        held = (slice(None), index, pl.ds(piece * PIECE, PIECE))
        return pltpu.make_async_remote_copy(
            src_ref=dens.at[held],
            dst_ref=other.at[held],
            send_sem=sys_send.at[index],
            recv_sem=sys_recv.at[index],
            device_id={"sys": 1 - sys_index},
            device_id_type=pl.DeviceIdType.MESH,
        )

    barrier = pltpu.get_barrier_semaphore()

    @pl.loop(1, count)
    def _(offset):
        pl.semaphore_signal(
            barrier, inc=1, device_id={"rc": peer(offset)}, device_id_type=pl.DeviceIdType.MESH
        )

    pl.semaphore_signal(
        barrier, inc=1, device_id={"sys": 1 - sys_index}, device_id_type=pl.DeviceIdType.MESH
    )
    pl.semaphore_wait(barrier, count)

    def send(chunk):
        forward_own(chunk).start()

        @pl.loop(1, count)
        def _(offset):
            forward(chunk, peer(offset), me).start()

            @pl.when(offset <= half // PIECE)
            def _():
                swap_piece(chunk, offset - 1).start()

    @pl.loop(0, AHEAD)
    def _(chunk):
        send(chunk)

    level_copy = pltpu.make_async_remote_copy(
        src_ref=dens.at[:, shared],
        dst_ref=level.at[:, odd],
        send_sem=level_sem.at[0],
        recv_sem=level_sem.at[1],
        device_id={"rc": partner},
        device_id_type=pl.DeviceIdType.MESH,
    )
    level_copy.start()
    level_own = pltpu.make_async_copy(dens.at[:, shared], level.at[:, odd], level_sem.at[2])
    level_own.start()
    mine_copy = pltpu.make_async_copy(dens, mine, mine_sem)
    mine_copy.start()

    my_part = me // (row_blocks * parts)
    my_row = lax.rem(me // parts, row_blocks) * ROWS
    left_mat[...] = ladder_matrix(
        left_ham[...], left_coupling[...], left_strength[...], sys_index * local + my_row
    )
    for block in range(row_blocks):
        right_mat[block] = ladder_matrix(
            right_ham[...],
            right_coupling[...],
            right_strength[...],
            sys_index * local + block * ROWS,
        )
    sys_mat[...] = system_matrix(system_real[...], system_imag[...], sys_index, local)

    mine_copy.wait()
    level_own.wait()
    level_copy.wait()
    full_levels = halves // 2

    @pl.loop(0, 2)
    def _(part):
        sign = jnp.where(part == 1, 1.0, -1.0)
        for block in range(row_blocks):
            row = pl.ds(block * ROWS, ROWS)

            @pl.loop(0, full_levels)
            def _(number):
                first = odd + 2 * number
                held = mine[part, pl.ds(first, 2), :, row, :].reshape(levels * ROWS, columns)
                term = product(right_mat[block], held) * sign
                rest[1 - part, pl.ds(first, 2), :, row, :] = term.reshape(2, half, ROWS, columns)

            held = level[part, :, :, row, :].reshape(levels * ROWS, columns)
            rows = pl.ds(pl.multiple_of(odd * half * ROWS, half * ROWS), half * ROWS)
            term = product(right_mat[block, rows, :], held) * sign
            rest[1 - part, shared, :, row, :] = term.reshape(half, ROWS, columns)

    def system_rows(index):
        swap(index).wait_recv()

        @pl.loop(0, half)
        def _(at):
            pair = (me * halves + index) * half + at
            damping = 0.5 * (left_damping[pair // levels] + right_damping[lax.rem(pair, levels)])
            real, imag = mine[0, index, at], mine[1, index, at]
            held = jnp.concatenate([real, imag, other[0, index, at], other[1, index, at]], axis=0)
            term = product(sys_mat[...], held)
            real, imag = real.astype(jnp.float32), imag.astype(jnp.float32)
            energy = energies[...]
            new_real = term[:local] + rest[0, index, at] - energy * imag - damping * real
            new_imag = term[local:] + rest[1, index, at] + energy * real - damping * imag
            rest[0, index, at] = new_real
            rest[1, index, at] = new_imag

    my_sign = jnp.where(my_part == 1, 1.0, -1.0)

    @pl.loop(0, chunks)
    def _(chunk):
        forward_own(chunk).wait()

        @pl.loop(1, count)
        def _(offset):
            forward(chunk, me, peer(offset)).wait_recv()

        @pl.when(chunk + AHEAD < chunks)
        def _():
            send(chunk + AHEAD)

        for side in range(2):
            held = jnp.concatenate(
                [taken[chunk, 2 * number + side] for number in range(levels)], axis=0
            )
            term = (product(left_mat[...], held) * my_sign).astype(jnp.bfloat16)
            for number in range(levels):
                given[chunk, 2 * number + side] = term[number * ROWS : (number + 1) * ROWS]
        giveback_own(chunk).start()

        @pl.loop(1, count)
        def _(offset):
            giveback(chunk, peer(offset), me).start()

        @pl.when(chunk > 0)
        def _():
            system_rows(chunk - 1)

    @pl.loop(chunks, halves)
    def _(index):
        swap(index).start()

    @pl.loop(chunks - 1, halves)
    def _(index):
        system_rows(index)

    @pl.loop(0, halves)
    def _(index):
        swap(index).wait_send()

    @pl.loop(0, chunks)
    def _(chunk):
        giveback_own(chunk).wait()

        @pl.loop(1, count)
        def _(offset):
            rank = peer(offset)
            forward(chunk, rank, me).wait_send()
            giveback(chunk, rank, me).wait_send()
            giveback(chunk, me, rank).wait_recv()


def add_kernel(rest, left, total, staged, sems):
    _, halves = rest.shape[:2]

    def out(part, index):
        return pltpu.make_async_copy(
            staged.at[part, index], total.at[part, index], sems.at[part, index]
        )

    for part in range(2):

        @pl.loop(0, halves)
        def _(index):
            summed = rest[part, index] + left[part, index].astype(jnp.float32)
            staged[part, index] = summed.astype(jnp.bfloat16)
            out(part, index).start()

    for part in range(2):

        @pl.loop(0, halves)
        def _(index):
            out(part, index).wait()


def exchanged(
    density,
    system_real,
    system_imag,
    left_ham,
    left_coupling,
    right_ham,
    right_coupling,
    left_strength,
    right_strength,
    left_damping,
    right_damping,
    energies,
):
    count = lax.axis_size("rc")
    levels = left_ham.shape[0]
    half = levels // 2
    _, local, pairs, columns = density.shape
    halves = pairs // half
    size = levels * ROWS
    row_blocks = local // ROWS
    chunks = half * 2 * row_blocks // count
    dens = jnp.transpose(density, (0, 2, 1, 3)).reshape(2, halves, half, local, columns)
    whole = pl.BlockSpec(memory_space=pltpu.VMEM)
    scalars = pl.BlockSpec(memory_space=pltpu.SMEM)
    anywhere = pl.BlockSpec(memory_space=pl.ANY)
    slab = jax.ShapeDtypeStruct(dens.shape, jnp.bfloat16)
    rest, left = pl.pallas_call(
        functools.partial(section_kernel, count),
        out_shape=[
            pltpu.VMEM(dens.shape, jnp.float32),
            pltpu.VMEM(dens.shape, jnp.bfloat16),
        ],
        in_specs=[anywhere] + [whole] * 8 + [scalars] * 2 + [whole],
        out_specs=[whole, whole],
        scratch_shapes=[
            pltpu.VMEM(dens.shape, jnp.bfloat16),
            pltpu.VMEM(dens.shape, jnp.bfloat16),
            pltpu.VMEM((2, 2, half, local, columns), jnp.bfloat16),
            pltpu.VMEM((chunks, count * halves, ROWS, columns), jnp.bfloat16),
            pltpu.VMEM((chunks, count * halves, ROWS, columns), jnp.bfloat16),
            pltpu.VMEM((size, size), jnp.bfloat16),
            pltpu.VMEM((row_blocks, size, size), jnp.bfloat16),
            pltpu.VMEM((2 * local, 4 * local), jnp.bfloat16),
            pltpu.SemaphoreType.DMA((chunks, count)),
            pltpu.SemaphoreType.DMA((chunks, count)),
            pltpu.SemaphoreType.DMA((chunks, count)),
            pltpu.SemaphoreType.DMA((chunks, count)),
            pltpu.SemaphoreType.DMA((halves,)),
            pltpu.SemaphoreType.DMA((halves,)),
            pltpu.SemaphoreType.DMA((3,)),
            pltpu.SemaphoreType.DMA,
        ],
        compiler_params=pltpu.CompilerParams(
            collective_id=0, has_side_effects=True, vmem_limit_bytes=41 * 2**20
        ),
        cost_estimate=pl.CostEstimate(
            flops=10 * 10**9, bytes_accessed=5 * dens.size * 2, transcendentals=0
        ),
    )(
        dens,
        system_real,
        system_imag,
        left_ham,
        left_coupling,
        right_ham,
        right_coupling,
        left_strength[None, :],
        right_strength[None, :],
        left_damping,
        right_damping,
        energies[None, :],
    )
    total = pl.pallas_call(
        add_kernel,
        out_shape=slab,
        in_specs=[whole, whole],
        out_specs=anywhere,
        scratch_shapes=[
            pltpu.VMEM(dens.shape, jnp.bfloat16),
            pltpu.SemaphoreType.DMA((2, halves)),
        ],
        compiler_params=pltpu.CompilerParams(vmem_limit_bytes=12 * 2**20),
        cost_estimate=pl.CostEstimate(
            flops=dens.size, bytes_accessed=dens.size * 2, transcendentals=0
        ),
    )(rest, left)
    return jnp.transpose(total.reshape(2, pairs, local, columns), (0, 2, 1, 3))


def fits(mesh, shapes):
    count, sides = mesh.shape["rc"], mesh.shape["sys"]
    _, states, pairs, columns = shapes[0]
    levels = shapes[3][0]
    if sides != 2 or levels % 2 or pairs % count or states % (2 * ROWS) or columns % LANES:
        return False
    half, local_pairs = levels // 2, pairs // count
    row_parts = 2 * (states // (2 * ROWS))
    if half % PIECE or half // PIECE >= count:
        return False
    if count % row_parts or half % (count // row_parts) or local_pairs % half:
        return False
    halves, chunks = local_pairs // half, half * row_parts // count
    return halves % 2 == 1 and halves >= chunks >= AHEAD


def solution(mesh):
    placed = (P(None, "sys", "rc", None), P(), P(), P(), P(), P(), P(), P(), P(), P(), P(), P())

    def run(*arrays):
        body = exchanged if fits(mesh, [array.shape for array in arrays]) else shards
        return jax.shard_map(
            body, mesh=mesh, in_specs=placed, out_specs=P(None, "sys", "rc", None), check_vma=False
        )(*arrays)

    return run
```
